512 devices in a mesh: seq: 128 (over z, y, core), head: 4 (over x).
Axes of the slice: x: 4, y: 4, z: 16, core: 2. Of those that a mesh axis runs over, the one named last changes fastest.
Arguments:
- tile_rows: bfloat16 [65536, 768], P('seq'), may hold values from -16 to 16
- tissue_mask: int32 [65536], replicated, may hold values 0 or 1
- slide_lengths: int32 [8], replicated, may hold values from 1 to 16384, 65536 in all
- region_rows: bfloat16 [4096, 768], P('seq'), may hold values from -6 to 6
- parent_lists: int32 [4096, 16], P('seq'), may hold values from 0 to 65535, as said below
- child_counts: int32 [4096], P('seq'), may hold values from 0 to 16, as said below
- region_cotangent: bfloat16 [4096, 768], P('seq'), may hold values from -6 to 6
- w_query: bfloat16 [768, 768], P(None, 'head'), may hold values from -0.21875 to 0.21875
- w_key: bfloat16 [768, 768], P(None, 'head'), may hold values from -0.21875 to 0.21875
- w_value: bfloat16 [768, 768], P(None, 'head'), may hold values from -0.21875 to 0.21875
- w_output: bfloat16 [768, 768], P('head'), may hold values from -0.21875 to 0.21875
- w_cross_query: bfloat16 [768, 768], P(None, 'head'), may hold values from -0.21875 to 0.21875
- w_cross_output: bfloat16 [768, 768], P('head'), may hold values from -0.21875 to 0.21875
Outputs:
- tile_output: bfloat16 [65536, 768], P('seq', 'head')
- region_output: bfloat16 [4096, 768], P('seq', 'head')
- value_grad: bfloat16 [65536, 768], P('seq', 'head')
The draws below stay inside these ranges and needn't reach their ends.
Inputs may be any that keep to these rules, and one draw needn't show every extreme that they name: `parent_lists`: every entry of row r lies within 128 positions of the tiles 512 * (r // 32) to 512 * (r // 32 + 1) - 1; only the first child_counts[r] entries are children, later entries are ignored. `child_counts`: the first and the last region of every block of 32 regions have 16 children.
All inputs are finite; a program needn't handle non-finite values.
Results may differ from the reference program's by a relative error of at most 0.019.
Values may be sent and summed in bfloat16 or wider, within the bound.
A program may use at most 64 MiB of HBM per device.

```python
import math
import jax
import jax.numpy as jnp
import numpy as np
from jax import lax

D = 768
HEADS = 12
HD = 64
KIDS = 16
SLIDES = 8
TOK_DEV = 512
TILES = 65536
REG_DEV = 32
REGIONS = 4096
REACH = 128
GRIDW = 64
N_SEQ = 128


def draw_tile_rows(key, part):
    normal_key = jax.random.fold_in(key, 3)
    values = jax.random.normal(normal_key, (TILES, D), jnp.float32)
    return jnp.clip(values, -6.0, 6.0).astype(jnp.bfloat16)


def parent_table(key):
    order_key = jax.random.fold_in(key, 17)
    count_key = jax.random.fold_in(key, 29)
    region_ids = jnp.arange(REGIONS, dtype=jnp.int32)
    owner_block = region_ids // REG_DEV
    within = region_ids % REG_DEV
    home = owner_block * TOK_DEV + within * (TOK_DEV // REG_DEV)
    slot_ids = jnp.arange(KIDS, dtype=jnp.int32)
    grid_row = slot_ids // 4
    grid_col = slot_ids % 4
    centred = home[:, None] + (grid_row[None, :] - 2) * GRIDW + grid_col[None, :]
    block_last = (owner_block + 1) * TOK_DEV - 1
    far_right = block_last[:, None] + REACH - (3 - grid_row[None, :]) * GRIDW - (3 - grid_col[None, :])
    is_last = (within == REG_DEV - 1)[:, None]
    candidates = jnp.where(is_last, far_right, centred)
    candidates = jnp.clip(candidates, 0, TILES - 1)
    ranking = jax.random.randint(order_key, (REGIONS, KIDS), 0, 1048576) * KIDS + slot_ids[None, :]
    order = jnp.argsort(ranking, axis=1)
    shuffled = jnp.take_along_axis(candidates, order, axis=1)
    counts = jax.random.randint(count_key, (REGIONS,), 0, KIDS + 1)
    counts = jnp.where((within == 0) | (within == REG_DEV - 1), KIDS, counts)
    return (shuffled.astype(jnp.int32), counts.astype(jnp.int32))


def draw_parent_lists(key, part):
    return parent_table(key)[0]


def draw_child_counts(key, part):
    return parent_table(key)[1]


def with_ends(result, key, smallest, high):
    index_at = [jax.random.randint(jax.random.fold_in(key, axis), (), 0, length) for axis, length in enumerate(result.shape)]
    main_axis = result.shape.index(max(result.shape))
    next_to = index_at[:main_axis] + [(index_at[main_axis] + 1) % result.shape[main_axis]] + index_at[main_axis + 1:]
    return result.at[tuple(index_at)].set(smallest).at[tuple(next_to)].set(high)


def block_scale(stream_key, dims, split, least, high):
    loudness = 1.0
    for position, shards_of in split:
        heights = jax.random.uniform(jax.random.fold_in(jax.random.fold_in(stream_key, 6), position), (shards_of,), jnp.float32, least / len(split), high / len(split))
        loudness = loudness * jnp.repeat(jnp.exp(heights), dims[position] // shards_of).reshape((-1,) + (1,) * (len(dims) - 1 - position))
    return loudness


def split_up(amount, total, reach, lean):
    weights = [(1 << 20) // math.isqrt(rank ** lean) + 1 for rank in range(2, amount + 1)]
    rest, given = total - reach - (amount - 1), [1] * (amount - 1)
    while rest > 0:
        free = [i for i in range(amount - 1) if given[i] < reach]
        mass, remaining = sum([weights[i] for i in free]), rest
        for i in free:
            addition = min(reach - given[i], max(1, remaining * weights[i] // mass), rest)
            given[i] = given[i] + addition
            rest = rest - addition
    return np.array([reach] + given)


def uneven(rng, count, total, most, skew):
    if count == 2:
        one = jax.random.randint(rng, (), max(1, total - most), min(most, total - 1) + 1)
        return jnp.stack([one, total - one])
    sizes = jnp.asarray(split_up(count, total, most, skew), jnp.int32)
    pairs = (count - 1) // 2
    source_of, sink = sizes[1:1 + 2 * pairs:2], sizes[2:2 + 2 * pairs:2]
    slack = jnp.minimum(source_of - 1, most - sink)
    shifted = jax.random.randint(jax.random.fold_in(rng, 1), (pairs,), 0, 1 << 20) % (slack + 1)
    sizes = sizes.at[1:1 + 2 * pairs:2].set(source_of - shifted).at[2:2 + 2 * pairs:2].set(sink + shifted)
    return sizes[jax.random.permutation(jax.random.fold_in(rng, 2), count)]


def normal_values(stream_key, extent, width, bound, cuts=(), kind=jnp.bfloat16):
    entries = width * jax.random.normal(stream_key, extent, jnp.float32)
    if cuts:
        entries = entries * block_scale(stream_key, extent, cuts, -0.22, 0.18)
    return jnp.clip(entries, -bound, bound).astype(kind)


def setup_inputs(seed: int = 0) -> dict:
    splits = jax.random.split(jax.random.key(seed), 14)
    return {
        "tile_rows": draw_tile_rows(jax.random.fold_in(splits[13], 71), 0),
        "tissue_mask": with_ends((jax.random.randint(splits[1], (TILES,), 0, 4) < 3).astype(jnp.int32), jax.random.fold_in(splits[1], 1), 0, 1),
        "slide_lengths": uneven(splits[2], SLIDES, TILES, TILES // 4, 2).astype(jnp.int32),
        "region_rows": normal_values(splits[3], (REGIONS, D), 1.0, 6.0, ((0, 128),)),
        "parent_lists": draw_parent_lists(jax.random.fold_in(splits[13], 71), 0),
        "child_counts": draw_child_counts(jax.random.fold_in(splits[13], 71), 0),
        "region_cotangent": normal_values(splits[6], (REGIONS, D), 1.0, 6.0, ((0, 128),)),
        "w_query": normal_values(splits[7], (D, D), D ** -0.5, 0.21875, ((1, 4),)),
        "w_key": normal_values(splits[8], (D, D), D ** -0.5, 0.21875, ((1, 4),)),
        "w_value": normal_values(splits[9], (D, D), D ** -0.5, 0.21875, ((1, 4),)),
        "w_output": normal_values(splits[10], (D, D), D ** -0.5, 0.21875, ((0, 4),)),
        "w_cross_query": normal_values(splits[11], (D, D), D ** -0.5, 0.21875, ((1, 4),)),
        "w_cross_output": normal_values(splits[12], (D, D), D ** -0.5, 0.21875, ((0, 4),)),
    }


def slide_index(positions, slide_lengths):
    slide_ends = jnp.cumsum(slide_lengths)
    return jnp.sum((positions[:, None] >= slide_ends[None, :]).astype(jnp.int32), axis=1)


def reference(tile_rows, tissue_mask, slide_lengths, region_rows, parent_lists, child_counts, region_cotangent, w_query, w_key, w_value, w_output, w_cross_query, w_cross_output):
    score_scale = HD ** -0.5
    query_all = jnp.dot(tile_rows, w_query, preferred_element_type=jnp.float32).astype(jnp.bfloat16)
    key_all = jnp.dot(tile_rows, w_key, preferred_element_type=jnp.float32).astype(jnp.bfloat16)
    value_all = jnp.dot(tile_rows, w_value, preferred_element_type=jnp.float32).astype(jnp.bfloat16)
    positions = jnp.arange(TILES, dtype=jnp.int32)
    slide_ids = slide_index(positions, slide_lengths)

    def strided(array):
        return jnp.swapaxes(array.reshape((TOK_DEV, N_SEQ) + array.shape[1:]), 0, 1)

    order_rows = jnp.arange(TOK_DEV, dtype=jnp.int32)
    offsets = order_rows[:, None] - order_rows[None, :]
    dilation = jnp.left_shift(jnp.ones((HEADS,), jnp.int32), jnp.arange(HEADS, dtype=jnp.int32) % 4)
    stride_ok = jnp.mod(offsets[None, :, :], dilation[:, None, None]) == 0

    def owner(pieces):
        query_rows, key_rows, value_rows, slide_rows, tissue_rows = pieces
        query_f = query_rows.astype(jnp.float32).reshape(TOK_DEV, HEADS, HD)
        key_f = key_rows.astype(jnp.float32).reshape(TOK_DEV, HEADS, HD)
        value_f = value_rows.astype(jnp.float32).reshape(TOK_DEV, HEADS, HD)
        scores = jnp.einsum("thd,uhd->htu", query_f, key_f) * score_scale
        allowed = (slide_rows[:, None] == slide_rows[None, :]) & ((tissue_rows[None, :] == 1) | (offsets == 0))
        allowed = allowed[None, :, :] & stride_ok
        highest = jnp.max(jnp.where(allowed, scores, -1e30), axis=2, keepdims=True)
        expon = jnp.where(allowed, jnp.exp(scores - highest), 0.0)
        weights = (expon / jnp.sum(expon, axis=2, keepdims=True)).astype(jnp.bfloat16)
        mixed = jnp.einsum("htu,uhd->thd", weights.astype(jnp.float32), value_f)
        return mixed.reshape(TOK_DEV, D).astype(jnp.bfloat16)

    attended = lax.map(owner, (strided(query_all), strided(key_all), strided(value_all), strided(slide_ids), strided(tissue_mask)))
    attended = jnp.swapaxes(attended, 0, 1).reshape(TILES, D)
    tile_output = jnp.dot(attended, w_output, preferred_element_type=jnp.float32).astype(jnp.bfloat16)

    cross_query = jnp.dot(region_rows, w_cross_query, preferred_element_type=jnp.float32).astype(jnp.bfloat16)
    region_keys = jnp.dot(region_rows, w_key, preferred_element_type=jnp.float32).astype(jnp.bfloat16)
    region_values = jnp.dot(region_rows, w_value, preferred_element_type=jnp.float32).astype(jnp.bfloat16)
    query_f = cross_query.astype(jnp.float32).reshape(REGIONS, HEADS, HD)
    own_key = region_keys.astype(jnp.float32).reshape(REGIONS, HEADS, HD)
    own_value = region_values.astype(jnp.float32).reshape(REGIONS, HEADS, HD)
    child_key = key_all[parent_lists].astype(jnp.float32).reshape(REGIONS, KIDS, HEADS, HD)
    child_value = value_all[parent_lists].astype(jnp.float32).reshape(REGIONS, KIDS, HEADS, HD)
    own_score = jnp.sum(query_f * own_key, axis=2)[:, :, None] * score_scale
    child_score = jnp.einsum("rhd,rkhd->rhk", query_f, child_key) * score_scale
    scores = jnp.concatenate([own_score, child_score], axis=2)
    valid = jnp.arange(KIDS, dtype=jnp.int32)[None, :] < child_counts[:, None]
    valid = jnp.concatenate([jnp.ones((REGIONS, 1), bool), valid], axis=1)[:, None, :]
    highest = jnp.max(jnp.where(valid, scores, -1e30), axis=2, keepdims=True)
    expon = jnp.where(valid, jnp.exp(scores - highest), 0.0)
    cross_weights = (expon / jnp.sum(expon, axis=2, keepdims=True)).astype(jnp.bfloat16)
    weight_f = cross_weights.astype(jnp.float32)
    mixed = weight_f[:, :, 0:1] * own_value + jnp.einsum("rhk,rkhd->rhd", weight_f[:, :, 1:], child_value)
    cross_attended = mixed.reshape(REGIONS, D).astype(jnp.bfloat16)
    region_output = jnp.dot(cross_attended, w_cross_output, preferred_element_type=jnp.float32).astype(jnp.bfloat16)

    back_signal = jnp.dot(region_cotangent, jnp.transpose(w_cross_output), preferred_element_type=jnp.float32)
    back_signal = back_signal.reshape(REGIONS, HEADS, HD)
    terms = jnp.transpose(weight_f[:, :, 1:], (0, 2, 1))[:, :, :, None] * back_signal[:, None, :, :]
    value_grad = jnp.zeros((TILES, D), jnp.float32).at[parent_lists.reshape(-1)].add(terms.reshape(REGIONS * KIDS, D))
    return tile_output, region_output, value_grad.astype(jnp.bfloat16)
```

```python
import functools

import jax
import jax.numpy as jnp
from jax import lax
from jax.experimental import pallas as pl
from jax.experimental.pallas import tpu as pltpu
from jax.sharding import PartitionSpec as P

HD = 64
NZ = 16
NQ = 8
NX = 4
MESH = pl.DeviceIdType.MESH
F32 = jnp.float32
BF16 = jnp.bfloat16
NEG = -1e30
ZORDER = (1, 15, 2, 14, 3, 13, 4, 12, 5, 11, 6, 10, 7, 9, 8)


def iota(shape, dim):
    return lax.broadcasted_iota(jnp.int32, shape, dim)


def nt(a, b):
    return lax.dot_general(a, b, (((1,), (1,)), ((), ())), preferred_element_type=F32)


def tn(a, b):
    return lax.dot_general(a, b, (((0,), (0,)), ((), ())), preferred_element_type=F32)


def mm(a, b):
    return jnp.dot(a, b, preferred_element_type=F32)


def order_of(row):
    return (row & ~31) | ((row & 7) << 2) | ((row >> 3) & 3)


def kernel(
    lengths,
    tiles,
    tissue,
    regions,
    parents,
    counts,
    cotangent,
    w_all,
    w_cq,
    wo4,
    wco4,
    wco,
    out_tile,
    out_region,
    out_grad,
    first,
    second,
    feats,
    qkv,
    ext,
    wrecv,
    wlast,
    att,
    zout,
    zin,
    pout,
    pin,
    gext,
    gown,
    gprev,
    gnext,
    rout,
    rin,
    perm_a,
    perm_b,
    p1s,
    p1r,
    p2s,
    p2r,
    pxs,
    pxr,
    wos,
    wor,
    has,
    har,
    axs,
    axr,
    zas,
    zar,
    pbs,
    pbr,
    grs,
    grr,
    res,
    rer,
):
    s = lax.axis_index("seq")
    x = lax.axis_index("head")
    z = s // NQ
    q = lax.rem(s, NQ)
    n_seq = NZ * NQ
    after = lax.rem(s + 1, n_seq)
    before = lax.rem(s + n_seq - 1, n_seq)

    def remote(src, dst, ss, rs, seq, head):
        return pltpu.make_async_remote_copy(
            src_ref=src,
            dst_ref=dst,
            send_sem=ss,
            recv_sem=rs,
            device_id={"seq": seq, "head": head},
            device_id_type=MESH,
        )

    sent = []

    def go(*args):
        copy = remote(*args)
        copy.start()
        sent.append(copy)
        return copy

    barrier = pltpu.get_barrier_semaphore()

    def greet(seq, head):
        pl.semaphore_signal(
            barrier, inc=1, device_id={"seq": seq, "head": head}, device_id_type=MESH
        )

    for d in range(1, NQ):
        greet(z * NQ + lax.rem(q + d, NQ), x)
    for d in ZORDER:
        greet(lax.rem(z + d, NZ) * NQ + q, x)
    for d in range(1, NX):
        greet(s, lax.rem(x + d, NX))
    greet(after, x)
    greet(before, x)
    pl.semaphore_wait(barrier, (NQ - 1) + (NZ - 1) + (NX - 1) + 2)

    hop1 = []
    for d in range(1, NQ):
        to = lax.rem(q + d, NQ)
        hop1.append(
            go(
                tiles.at[pl.ds(pl.multiple_of(x * 128 + to * 16, 16), 16)],
                first.at[pl.ds(pl.multiple_of(q * 16, 16), 16)],
                p1s.at[d],
                p1r.at[d],
                z * NQ + to,
                x,
            )
        )
    first[pl.ds(pl.multiple_of(q * 16, 16), 16), :] = tiles[
        pl.ds(pl.multiple_of(x * 128 + q * 16, 16), 16), :
    ]
    wcopies = []
    for d in range(1, NX):
        to = lax.rem(x + d, NX)
        wcopies.append(go(wo4.at[to], wrecv.at[x], wos.at[d], wor.at[d], s, to))
    wrecv[x] = wo4[x]

    block = tiles[...]
    ext[128:640, 0:256] = mm(block, w_all[:, 128:384]).astype(BF16)
    ext[128:640, 256:384] = mm(block, w_all[:, 512:640]).astype(BF16)
    halos = [
        go(ext.at[128:256], ext.at[640:768], has.at[0], har.at[0], before, x),
        go(ext.at[512:640], ext.at[0:128], has.at[1], har.at[1], after, x),
    ]

    lane = iota((256, 128), 1)
    row = iota((256, 128), 0)
    source = (lane & 15) * 16 + (lane >> 4)
    left = (source == row).astype(BF16)
    right = (source + 8 == row).astype(BF16)
    for copy in hop1:
        copy.wait_recv()
    second[...] = (
        (mm(left, first[:, 0:384]) + mm(right, first[:, 384:768]))
        .astype(BF16)
        .reshape(NZ, 16, 384)
    )
    hop2 = {}
    for d in ZORDER:
        to = lax.rem(z + d, NZ)
        hop2[d] = go(second.at[to], feats.at[z, x], p2s.at[d], p2r.at[d], to * NQ + q, x)
    feats[z, x] = second[z]

    hopx = []

    def spread(d):
        at = lax.rem(z - d + NZ, NZ)
        for e in range(1, NX):
            to = lax.rem(x + e, NX)
            hopx.append(
                go(feats.at[at, x], feats.at[at, x], pxs.at[e, d], pxr.at[e, d], s, to)
            )

    spread(0)
    for d in ZORDER:
        hop2[d].wait_recv()
        spread(d)

    low = iota((32, 128), 1) < HD
    rows32 = regions[...]
    cq = (mm(rows32, w_cq[...]).astype(BF16)).astype(F32) * (HD**-0.5)
    rk = mm(rows32, w_all[:, 128:384]).astype(BF16).astype(F32)
    rkv2 = mm(rows32, w_all[:, 512:640]).astype(BF16).astype(F32)
    rk01, rv01 = rk[:, 0:128], rk[:, 128:256]
    cq0 = jnp.where(low, cq[:, 0:128], 0.0)
    cq1 = jnp.where(low, 0.0, cq[:, 0:128])
    cq2 = jnp.where(low, cq[:, 128:256], 0.0)
    back = nt(cotangent[...], wco[...]).astype(BF16)
    place = iota((32, 768), 1)
    times = jnp.zeros((32, 768), F32)
    base = s * 512 - 128
    count = counts[...]
    lists = parents[...] - base
    for j in range(16):
        hit = (lists[:, j : j + 1] == place) & (j < count)
        times = times + jnp.where(hit, 1.0, 0.0)
    valid = times > 0.0
    for copy in halos:
        copy.wait_recv()
    outs = []
    grads = []
    for h in range(3):
        query = (cq0, cq1, cq2)[h]
        own = jnp.sum(query * (rk01 if h < 2 else rkv2), axis=1, keepdims=True)
        keys = ext[:, 0:128] if h < 2 else ext[:, 256:384]
        values = ext[:, 128:256] if h < 2 else keys
        sc = jnp.where(valid, nt(query.astype(BF16), keys), NEG)
        top = jnp.maximum(own, jnp.max(sc, axis=1, keepdims=True))
        ex = jnp.where(valid, jnp.exp(sc - top), 0.0)
        ex_own = jnp.exp(own - top)
        total = ex_own + jnp.sum(times * ex, axis=1, keepdims=True)
        weight = (ex / total).astype(BF16).astype(F32)
        weight_own = (ex_own / total).astype(BF16).astype(F32)
        mixed = (times * weight).astype(BF16)
        outs.append(mm(mixed, values) + weight_own * (rv01 if h < 2 else rkv2))
        grads.append(tn(mixed, back[:, 0:128] if h < 2 else back[:, 128:192]))
    cross_a = jnp.where(low, outs[0], outs[1]).astype(BF16)
    cross_b = pltpu.roll(outs[2], 64, 1)[:, 0:64].astype(BF16)
    low768 = iota((768, 128), 1) < HD
    grad_a = jnp.where(low768, grads[0], grads[1])
    grad_b = grads[2]
    gown[:, 0:128] = grad_a[128:640]
    gown[:, 128:192] = grad_b[128:640]
    zero = jnp.zeros((128, 64), BF16)
    gext[0:128, 0:128] = grad_a[0:128].astype(BF16)
    gext[0:128, 128:256] = jnp.concatenate([grad_b[0:128].astype(BF16), zero], axis=1)
    gext[128:256, 0:128] = grad_a[640:768].astype(BF16)
    gext[128:256, 128:256] = jnp.concatenate([grad_b[640:768].astype(BF16), zero], axis=1)
    gcopies = [
        go(gext.at[0:128], gnext, grs.at[0], grr.at[0], before, x),
        go(gext.at[128:256], gprev, grs.at[1], grr.at[1], after, x),
    ]
    for g in range(NX):
        rout[g] = (mm(cross_a, wco4[g, 0:128]) + mm(cross_b, wco4[g, 128:192])).astype(BF16)
    rcopies = []
    for d in range(1, NX):
        to = lax.rem(x + d, NX)
        rcopies.append(go(rout.at[to], rin.at[x], res.at[d], rer.at[d], s, to))
    rin[x] = rout[x]

    prow = iota((512, 512), 0)
    pcol = iota((512, 512), 1)
    perm_a[...] = (
        ((prow & 15) * 32 + ((prow >> 4) & 3) * 8 + (prow >> 6)) == pcol
    ).astype(BF16)
    prow = iota((256, 256), 0)
    pcol = iota((256, 256), 1)
    perm_b[...] = (
        ((prow & 15) * 16 + ((prow >> 4) & 1) * 8 + (prow >> 5)) == pcol
    ).astype(BF16)
    wlast[:, 0:64] = jnp.zeros((NX, 64, 256), BF16)
    wlast[:, 128:192] = jnp.zeros((NX, 64, 256), BF16)

    c = q * NZ + z
    pick = (iota((16, 128), 1) == c).astype(BF16)
    tissue_n = nt(pick, tissue[...].astype(F32).astype(BF16)).astype(BF16)
    spread_n = (iota((512, 512), 0) == order_of(iota((512, 512), 1))).astype(BF16)
    tissue_row = mm(tissue_n, spread_n)[0:1]
    n_row = order_of(iota((1, 512), 1))
    slide_row = jnp.zeros((1, 512), jnp.int32)
    end = jnp.int32(0)
    for k in range(8):
        end = end + lengths[k]
        slide_row = slide_row + jnp.where(n_row * 128 + c >= end, 1, 0)

    for copy in hopx:
        copy.wait_recv()

    for b in range(4):
        part = feats[4 * b : 4 * b + 4].astype(F32).reshape(16, 2, 8, 384)
        left = part[:, 0].reshape(128, 384).astype(BF16)
        right = part[:, 1].reshape(128, 384).astype(BF16)
        qkv[128 * b : 128 * b + 128] = (
            mm(left, w_all[0:384]) + mm(right, w_all[384:768])
        ).astype(BF16)

    low128 = iota((128, 128), 1) < HD
    keys01 = qkv[:, 128:256].astype(F32)
    low512 = iota((512, 128), 1) < HD
    key0 = jnp.where(low512, keys01, 0.0).astype(BF16)
    key1 = jnp.where(low512, 0.0, keys01).astype(BF16)
    key_value2 = qkv[:, 512:640]
    values01 = qkv[:, 256:384]
    has_tissue = tissue_row > 0.5
    own_chunk = z // 4
    low64 = iota((64, 128), 1) < HD

    acopies = {}
    for j in range(4):
        chunk = lax.rem(own_chunk + j, 4)
        at = pl.multiple_of(chunk * 128, 128)
        query01 = (qkv[pl.ds(at, 128), 0:128].astype(F32) * (HD**-0.5)).astype(BF16)
        query2 = (qkv[pl.ds(at, 128), 384:512].astype(F32) * (HD**-0.5)).astype(BF16)
        row = iota((128, 1), 0) + at
        n_mine = order_of(row)
        slide_mine = jnp.zeros((128, 1), jnp.int32)
        end = jnp.int32(0)
        for k in range(8):
            end = end + lengths[k]
            slide_mine = slide_mine + jnp.where(n_mine * 128 + c >= end, 1, 0)
        base_ok = (slide_mine == slide_row) & (has_tissue | (row == iota((128, 512), 1)))
        parts = []
        for h in range(3):
            step = (jnp.int32(1) << lax.rem(3 * x + h, 4)) - 1
            allowed = base_ok & ((n_mine & step) == (n_row & step))
            sc = nt(query01 if h < 2 else query2, (key0, key1, key_value2)[h])
            sc = jnp.where(allowed, sc, NEG)
            ex = jnp.exp(sc - jnp.max(sc, axis=1, keepdims=True))
            total = jnp.sum(ex, axis=1, keepdims=True)
            parts.append(mm(ex.astype(BF16), values01 if h < 2 else key_value2) / total)
        att[x, chunk, 0:128] = jnp.where(low128, parts[0], parts[1]).astype(BF16)
        att[x, chunk, 128:192] = jnp.where(
            low64, pltpu.roll(parts[2][0:64], 64, 1), parts[2][64:128]
        ).astype(BF16)
        for e in range(1, NX):
            to = lax.rem(x + e, NX)
            acopies[e, j] = go(
                att.at[x, chunk], att.at[x, chunk], axs.at[e, j], axr.at[e, j], s, to
            )
        if j == 0:
            for copy in wcopies:
                copy.wait_recv()
            wlast[:, 64:128] = wrecv[:, 128:192]
        if j > 0:
            finish(acopies, j - 1, own_chunk, att, wrecv, wlast, zout, low64)
            send_z(go, zout, zin, zas, zar, own_chunk, j - 1, z, q, x)
    finish(acopies, 3, own_chunk, att, wrecv, wlast, zout, low64)
    send_z(go, zout, zin, zas, zar, own_chunk, 3, z, q, x)
    zin[z] = zout[z]

    for copy in gcopies + rcopies:
        copy.wait_recv()
    gown[0:128, 0:192] = gown[0:128, 0:192] + gprev[:, 0:192].astype(F32)
    gown[384:512, 0:192] = gown[384:512, 0:192] + gnext[:, 0:192].astype(F32)
    out_grad[...] = gown[:, 0:192].astype(BF16)
    total = rin[0].astype(F32)
    for g in range(1, NX):
        total = total + rin[g].astype(F32)
    out_region[...] = total[:, 0:192].astype(BF16)

    for d in range(1, NZ):
        copy = remote(
            zout.at[z], zin.at[z], zas.at[d], zar.at[d], lax.rem(z + d, NZ) * NQ + q, x
        )
        copy.wait_recv()
        sent.append(copy)
    rows_a = mm(perm_a[...], zin[:, 0:32].reshape(512, 128)).astype(BF16)
    rows_b = mm(perm_b[...], zin[:, 32:48].reshape(256, 128)).astype(BF16)
    pout[:, 0:64] = rows_a.reshape(NQ, 64, 128)
    pout[:, 64:96] = rows_b.reshape(NQ, 32, 128)
    backs = []
    for d in range(1, NQ):
        to = lax.rem(q + d, NQ)
        backs.append(go(pout.at[to], pin.at[q], pbs.at[d], pbr.at[d], z * NQ + to, x))
    pin[q] = pout[q]
    for copy in backs:
        copy.wait_recv()
    for p in range(NQ):
        half = pin[p, 64:96].astype(F32)
        turned = pltpu.roll(half, 64, 1)
        for i in range(4):
            at = i * 128 + p * 16
            out_tile[at : at + 16, 0:128] = pin[p, 16 * i : 16 * i + 16]
            k = (i & 1) * 16
            out_tile[at : at + 16, 128:192] = (half if i < 2 else turned)[
                k : k + 16, 0:64
            ].astype(BF16)
    for copy in sent:
        copy.wait_send()


def finish(acopies, j, own_chunk, att, wrecv, wlast, zout, low64):
    for e in range(1, NX):
        acopies[e, j].wait_recv()
    chunk = lax.rem(own_chunk + j, 4)
    acc = jnp.zeros((128, 256), F32)
    upper = jnp.zeros((64, 256), F32)
    lower = jnp.zeros((64, 256), F32)
    for g in range(NX):
        acc = acc + mm(att[g, chunk, 0:128], wrecv[g, 0:128])
        upper = upper + mm(att[g, chunk, 128:192], wlast[g, 64:192])
        lower = lower + mm(att[g, chunk, 128:192], wlast[g, 0:128])
    acc = acc + jnp.concatenate([upper, lower], axis=0)
    two = acc[:, 128:256].reshape(4, 2, 16, 128)
    packed = jnp.where(
        low64,
        two[:, 0].reshape(64, 128),
        pltpu.roll(two[:, 1].reshape(64, 128), 64, 1),
    )
    at = chunk * 4
    zout[pl.ds(at, 4), 0:32] = acc[:, 0:128].reshape(4, 32, 128).astype(BF16)
    zout[pl.ds(at, 4), 32:48] = packed.reshape(4, 16, 128).astype(BF16)


def send_z(go, zout, zin, zas, zar, own_chunk, j, z, q, x):
    for k in range(4):
        to = lax.rem(own_chunk + j, 4) * 4 + k
        d = lax.rem(to - z + NZ, NZ)

        @pl.when(d != 0)
        def _():
            copy = pltpu.make_async_remote_copy(
                src_ref=zout.at[to],
                dst_ref=zin.at[z],
                send_sem=zas.at[d],
                recv_sem=zar.at[d],
                device_id={"seq": to * NQ + q, "head": x},
                device_id_type=MESH,
            )
            copy.start()


def body(
    tile_rows,
    tissue_mask,
    slide_lengths,
    region_rows,
    parent_lists,
    child_counts,
    region_cotangent,
    w_query,
    w_key,
    w_value,
    w_output,
    w_cross_query,
    w_cross_output,
):
    pad = ((0, 0), (0, 64))
    w_all = jnp.concatenate(
        [
            w_query[:, :128],
            w_key[:, :128],
            w_value[:, :128],
            jnp.pad(w_query[:, 128:], pad),
            w_key[:, 128:],
            w_value[:, 128:],
        ],
        axis=1,
    )
    w_cq = jnp.pad(w_cross_query, pad)
    split = lambda w: jnp.transpose(
        jnp.pad(w.reshape(192, NX, 192), ((0, 0), (0, 0), (0, 64))), (1, 0, 2)
    )
    dma = pltpu.SemaphoreType.DMA
    vmem = lambda *shape: pltpu.VMEM(shape, BF16)
    return pl.pallas_call(
        kernel,
        out_shape=(
            jax.ShapeDtypeStruct((512, 192), BF16),
            jax.ShapeDtypeStruct((32, 192), BF16),
            jax.ShapeDtypeStruct((512, 192), BF16),
        ),
        in_specs=[pl.BlockSpec(memory_space=pltpu.SMEM)]
        + [pl.BlockSpec(memory_space=pltpu.VMEM)] * 11,
        out_specs=(pl.BlockSpec(memory_space=pltpu.VMEM),) * 3,
        scratch_shapes=[
            vmem(128, 768),
            vmem(16, 16, 384),
            vmem(16, 4, 16, 384),
            vmem(512, 640),
            vmem(768, 384),
            vmem(4, 192, 256),
            vmem(4, 192, 256),
            vmem(4, 4, 192, 128),
            vmem(16, 48, 128),
            vmem(16, 48, 128),
            vmem(8, 96, 128),
            vmem(8, 96, 128),
            vmem(256, 256),
            pltpu.VMEM((512, 256), F32),
            vmem(128, 256),
            vmem(128, 256),
            vmem(4, 32, 256),
            vmem(4, 32, 256),
            vmem(512, 512),
            vmem(256, 256),
            dma((8,)),
            dma((8,)),
            dma((16,)),
            dma((16,)),
            dma((4, 16)),
            dma((4, 16)),
            dma((4,)),
            dma((4,)),
            dma((2,)),
            dma((2,)),
            dma((4, 4)),
            dma((4, 4)),
            dma((16,)),
            dma((16,)),
            dma((8,)),
            dma((8,)),
            dma((2,)),
            dma((2,)),
            dma((4,)),
            dma((4,)),
        ],
        compiler_params=pltpu.CompilerParams(
            collective_id=0, has_side_effects=True, vmem_limit_bytes=48 * 1024 * 1024
        ),
    )(
        slide_lengths,
        tile_rows,
        tissue_mask.reshape(512, 128),
        region_rows,
        parent_lists,
        child_counts.reshape(32, 1),
        region_cotangent,
        w_all,
        w_cq,
        split(w_output),
        split(w_cross_output),
        w_cross_output,
    )


def solution(mesh):
    in_specs = (
        P("seq", None),
        P(),
        P(),
        P("seq", None),
        P("seq", None),
        P("seq"),
        P("seq", None),
        P(None, "head"),
        P(None, "head"),
        P(None, "head"),
        P("head", None),
        P(None, "head"),
        P("head", None),
    )
    out_specs = (P("seq", "head"), P("seq", "head"), P("seq", "head"))
    return jax.shard_map(body, mesh=mesh, in_specs=in_specs, out_specs=out_specs, check_vma=False)
```

```python
import functools

import jax
import jax.numpy as jnp
from jax import lax
from jax.experimental import pallas as pl
from jax.experimental.pallas import tpu as pltpu
from jax.sharding import PartitionSpec as P

HD = 64
NZ = 16
NQ = 8
NX = 4
MESH = pl.DeviceIdType.MESH
F32 = jnp.float32
BF16 = jnp.bfloat16
NEG = -1e30
ZORDER = (1, 15, 2, 14, 3, 13, 4, 12, 5, 11, 6, 10, 7, 9, 8)


def iota(shape, dim):
    return lax.broadcasted_iota(jnp.int32, shape, dim)


def nt(a, b):
    return lax.dot_general(a, b, (((1,), (1,)), ((), ())), preferred_element_type=F32)


def tn(a, b):
    return lax.dot_general(a, b, (((0,), (0,)), ((), ())), preferred_element_type=F32)


def mm(a, b):
    return jnp.dot(a, b, preferred_element_type=F32)


def order_of(row):
    return (row & ~31) | ((row & 7) << 2) | ((row >> 3) & 3)


def kernel(
    lengths,
    tiles,
    tissue,
    regions,
    parents,
    counts,
    cotangent,
    wq_t,
    wk_t,
    wv_t,
    wo,
    wcq_t,
    wco,
    out_tile,
    out_region,
    out_grad,
    tiles_in,
    tissue_in,
    w_t,
    wo_in,
    wcq_in,
    wco_in,
    wout,
    first,
    second,
    feats,
    qkv,
    ext,
    wrecv,
    wlast,
    att,
    zout,
    zin,
    pout,
    pin,
    gext,
    gown,
    gprev,
    gnext,
    rout,
    rin,
    perm_a,
    perm_b,
    rows_out,
    loads,
    p1s,
    p1r,
    p2s,
    p2r,
    pxs,
    pxr,
    wos,
    wor,
    has,
    har,
    axs,
    axr,
    zas,
    zar,
    pbs,
    pbr,
    grs,
    grr,
    res,
    rer,
):
    s = lax.axis_index("seq")
    x = lax.axis_index("head")
    z = s // NQ
    q = lax.rem(s, NQ)
    n_seq = NZ * NQ
    after = lax.rem(s + 1, n_seq)
    before = lax.rem(s + n_seq - 1, n_seq)

    def remote(src, dst, ss, rs, seq, head):
        return pltpu.make_async_remote_copy(
            src_ref=src,
            dst_ref=dst,
            send_sem=ss,
            recv_sem=rs,
            device_id={"seq": seq, "head": head},
            device_id_type=MESH,
        )

    sent = []

    def go(*args):
        copy = remote(*args)
        copy.start()
        sent.append(copy)
        return copy

    local = []

    def load(src, dst):
        copy = pltpu.make_async_copy(src, dst, loads.at[len(local)])
        copy.start()
        local.append(copy)
        return copy

    load_tiles = load(tiles, tiles_in)
    load_w = [
        load(wk_t.at[0:128], w_t.at[128:256]),
        load(wv_t.at[0:128], w_t.at[256:384]),
        load(wk_t.at[128:192], w_t.at[512:576]),
        load(wv_t.at[128:192], w_t.at[576:640]),
        load(wq_t.at[0:128], w_t.at[0:128]),
        load(wq_t.at[128:192], w_t.at[384:448]),
    ]
    load_wo = load(wo, wo_in)
    load_wcq = load(wcq_t, wcq_in.at[0:192])
    load_wco = load(wco, wco_in)
    load_tissue = load(tissue, tissue_in)

    barrier = pltpu.get_barrier_semaphore()

    def greet(seq, head):
        pl.semaphore_signal(
            barrier, inc=1, device_id={"seq": seq, "head": head}, device_id_type=MESH
        )

    for d in range(1, NQ):
        greet(z * NQ + lax.rem(q + d, NQ), x)
    for d in ZORDER:
        greet(lax.rem(z + d, NZ) * NQ + q, x)
    for d in range(1, NX):
        greet(s, lax.rem(x + d, NX))
    greet(after, x)
    greet(before, x)
    pl.semaphore_wait(barrier, (NQ - 1) + (NZ - 1) + (NX - 1) + 2)

    hop1 = []
    for d in range(1, NQ):
        to = lax.rem(q + d, NQ)
        hop1.append(
            go(
                tiles.at[pl.ds(pl.multiple_of(x * 128 + to * 16, 16), 16)],
                first.at[pl.ds(pl.multiple_of(q * 16, 16), 16)],
                p1s.at[d],
                p1r.at[d],
                z * NQ + to,
                x,
            )
        )
    load_wo.wait()
    blocks_of(wo_in[...].astype(F32), wout)
    wcopies = []
    for d in range(1, NX):
        to = lax.rem(x + d, NX)
        wcopies.append(go(wout.at[to], wrecv.at[x], wos.at[d], wor.at[d], s, to))
    wrecv[x] = wout[x]

    load_tiles.wait()
    for copy in load_w:
        copy.wait()
    w_t[448:512] = jnp.zeros((64, 768), BF16)
    first[pl.ds(pl.multiple_of(q * 16, 16), 16), :] = tiles_in[
        pl.ds(pl.multiple_of(x * 128 + q * 16, 16), 16), :
    ]
    block = tiles_in[...]
    ext[128:640, 0:256] = nt(block, w_t[128:384]).astype(BF16)
    ext[128:640, 256:384] = nt(block, w_t[512:640]).astype(BF16)
    halos = [
        go(ext.at[128:256], ext.at[640:768], has.at[0], har.at[0], before, x),
        go(ext.at[512:640], ext.at[0:128], has.at[1], har.at[1], after, x),
    ]

    lane = iota((256, 128), 1)
    row = iota((256, 128), 0)
    source = (lane & 15) * 16 + (lane >> 4)
    left = (source == row).astype(BF16)
    right = (source + 8 == row).astype(BF16)
    for copy in hop1:
        copy.wait_recv()
    second[...] = (
        (mm(left, first[:, 0:384]) + mm(right, first[:, 384:768]))
        .astype(BF16)
        .reshape(NZ, 16, 384)
    )
    hop2 = {}
    for d in ZORDER:
        to = lax.rem(z + d, NZ)
        hop2[d] = go(second.at[to], feats.at[z, x], p2s.at[d], p2r.at[d], to * NQ + q, x)
    feats[z, x] = second[z]

    hopx = []

    def spread(d):
        at = lax.rem(z - d + NZ, NZ)
        for e in range(1, NX):
            to = lax.rem(x + e, NX)
            hopx.append(
                go(feats.at[at, x], feats.at[at, x], pxs.at[e, d], pxr.at[e, d], s, to)
            )

    spread(0)
    for d in ZORDER:
        hop2[d].wait_recv()
        spread(d)

    low = iota((32, 128), 1) < HD
    rows32 = regions[...]
    load_wcq.wait()
    load_wco.wait()
    wcq_in[192:256] = jnp.zeros((64, 768), BF16)
    cq = nt(rows32, wcq_in[...]).astype(BF16).astype(F32) * (HD**-0.5)
    rk = nt(rows32, w_t[128:384]).astype(BF16).astype(F32)
    rkv2 = nt(rows32, w_t[512:640]).astype(BF16).astype(F32)
    rk01, rv01 = rk[:, 0:128], rk[:, 128:256]
    cq0 = jnp.where(low, cq[:, 0:128], 0.0)
    cq1 = jnp.where(low, 0.0, cq[:, 0:128])
    cq2 = jnp.where(low, cq[:, 128:256], 0.0)
    back_t = nt(wco_in[...], cotangent[...]).astype(BF16)
    place = iota((32, 768), 1)
    times = jnp.zeros((32, 768), F32)
    base = s * 512 - 128
    lists = jnp.where(iota((16, 32), 0) < counts[...], parents[...] - base, -1)
    lists = jnp.transpose(lists.astype(F32)).astype(jnp.int32)
    for j in range(16):
        times = times + jnp.where(lists[:, j : j + 1] == place, 1.0, 0.0)
    valid = times > 0.0
    for copy in halos:
        copy.wait_recv()
    outs = []
    for h in range(3):
        query = (cq0, cq1, cq2)[h]
        own = jnp.sum(query * (rk01 if h < 2 else rkv2), axis=1, keepdims=True)
        keys = ext[:, 0:128] if h < 2 else ext[:, 256:384]
        values = ext[:, 128:256] if h < 2 else keys
        sc = jnp.where(valid, nt(query.astype(BF16), keys), NEG)
        top = jnp.maximum(own, jnp.max(sc, axis=1, keepdims=True))
        ex = jnp.where(valid, jnp.exp(sc - top), 0.0)
        ex_own = jnp.exp(own - top)
        total = ex_own + jnp.sum(times * ex, axis=1, keepdims=True)
        weight = (ex / total).astype(BF16).astype(F32)
        weight_own = (ex_own / total).astype(BF16).astype(F32)
        mixed = (times * weight).astype(BF16)
        outs.append(mm(mixed, values) + weight_own * (rv01 if h < 2 else rkv2))
        grad = mm(back_t[64 * h : 64 * h + 64], mixed)
        gown[64 * h : 64 * h + 64] = grad[:, 128:640]
        gext[0, 64 * h : 64 * h + 64] = grad[:, 0:128].astype(BF16)
        gext[1, 64 * h : 64 * h + 64] = grad[:, 640:768].astype(BF16)
    cross_a = jnp.where(low, outs[0], outs[1]).astype(BF16)
    cross_b = pltpu.roll(outs[2], 64, 1)[:, 0:64].astype(BF16)
    gcopies = [
        go(gext.at[0], gnext, grs.at[0], grr.at[0], before, x),
        go(gext.at[1], gprev, grs.at[1], grr.at[1], after, x),
    ]
    blocks_of(mm(cross_a, wco_in[0:128]) + mm(cross_b, wco_in[128:192]), rout)
    rcopies = []
    for d in range(1, NX):
        to = lax.rem(x + d, NX)
        rcopies.append(go(rout.at[to], rin.at[x], res.at[d], rer.at[d], s, to))
    rin[x] = rout[x]

    prow = iota((512, 512), 0)
    pcol = iota((512, 512), 1)
    perm_a[...] = (
        ((prow & 15) * 32 + ((prow >> 4) & 3) * 8 + (prow >> 6)) == pcol
    ).astype(BF16)
    prow = iota((256, 256), 0)
    pcol = iota((256, 256), 1)
    perm_b[...] = (
        ((prow & 15) * 16 + ((prow >> 4) & 1) * 8 + (prow >> 5)) == pcol
    ).astype(BF16)
    wlast[:, 0:64] = jnp.zeros((NX, 64, 256), BF16)
    wlast[:, 128:192] = jnp.zeros((NX, 64, 256), BF16)

    c = q * NZ + z
    load_tissue.wait()
    pick = (iota((16, 128), 1) == c).astype(BF16)
    tissue_n = nt(pick, tissue_in[...].astype(F32).astype(BF16)).astype(BF16)
    spread_n = (iota((512, 512), 0) == order_of(iota((512, 512), 1))).astype(BF16)
    tissue_row = mm(tissue_n, spread_n)[0:1]
    n_row = order_of(iota((1, 512), 1))
    slide_row = jnp.zeros((1, 512), jnp.int32)
    end = jnp.int32(0)
    for k in range(8):
        end = end + lengths[k]
        slide_row = slide_row + jnp.where(n_row * 128 + c >= end, 1, 0)

    for copy in hopx:
        copy.wait_recv()

    for b in range(4):
        part = feats[4 * b : 4 * b + 4].astype(F32).reshape(16, 2, 8, 384)
        left = part[:, 0].reshape(128, 384).astype(BF16)
        right = part[:, 1].reshape(128, 384).astype(BF16)
        qkv[128 * b : 128 * b + 128] = (
            nt(left, w_t[:, 0:384]) + nt(right, w_t[:, 384:768])
        ).astype(BF16)

    low128 = iota((128, 128), 1) < HD
    keys01 = qkv[:, 128:256].astype(F32)
    low512 = iota((512, 128), 1) < HD
    key0 = jnp.where(low512, keys01, 0.0).astype(BF16)
    key1 = jnp.where(low512, 0.0, keys01).astype(BF16)
    key_value2 = qkv[:, 512:640]
    values01 = qkv[:, 256:384]
    has_tissue = tissue_row > 0.5
    own_chunk = z // 4
    low64 = iota((64, 128), 1) < HD

    acopies = {}
    for j in range(4):
        chunk = lax.rem(own_chunk + j, 4)
        at = pl.multiple_of(chunk * 128, 128)
        query01 = (qkv[pl.ds(at, 128), 0:128].astype(F32) * (HD**-0.5)).astype(BF16)
        query2 = (qkv[pl.ds(at, 128), 384:512].astype(F32) * (HD**-0.5)).astype(BF16)
        row = iota((128, 1), 0) + at
        n_mine = order_of(row)
        slide_mine = jnp.zeros((128, 1), jnp.int32)
        end = jnp.int32(0)
        for k in range(8):
            end = end + lengths[k]
            slide_mine = slide_mine + jnp.where(n_mine * 128 + c >= end, 1, 0)
        base_ok = (slide_mine == slide_row) & (has_tissue | (row == iota((128, 512), 1)))
        parts = []
        for h in range(3):
            step = (jnp.int32(1) << lax.rem(3 * x + h, 4)) - 1
            allowed = base_ok & ((n_mine & step) == (n_row & step))
            sc = nt(query01 if h < 2 else query2, (key0, key1, key_value2)[h])
            sc = jnp.where(allowed, sc, NEG)
            ex = jnp.exp(sc - jnp.max(sc, axis=1, keepdims=True))
            total = jnp.sum(ex, axis=1, keepdims=True)
            parts.append(mm(ex.astype(BF16), values01 if h < 2 else key_value2) / total)
        att[x, chunk, 0:128] = jnp.where(low128, parts[0], parts[1]).astype(BF16)
        att[x, chunk, 128:192] = jnp.where(
            low64, pltpu.roll(parts[2][0:64], 64, 1), parts[2][64:128]
        ).astype(BF16)
        for e in range(1, NX):
            to = lax.rem(x + e, NX)
            acopies[e, j] = go(
                att.at[x, chunk], att.at[x, chunk], axs.at[e, j], axr.at[e, j], s, to
            )
        if j == 0:
            for copy in wcopies:
                copy.wait_recv()
            wlast[:, 64:128] = wrecv[:, 128:192]
        if j > 0:
            finish(acopies, j - 1, own_chunk, att, wrecv, wlast, zout, low64)
            send_z(go, zout, zin, zas, zar, own_chunk, j - 1, z, q, x)
    finish(acopies, 3, own_chunk, att, wrecv, wlast, zout, low64)
    send_z(go, zout, zin, zas, zar, own_chunk, 3, z, q, x)
    zin[z] = zout[z]

    for copy in gcopies + rcopies:
        copy.wait_recv()
    gown[:, 0:128] = gown[:, 0:128] + gprev[...].astype(F32)
    gown[:, 384:512] = gown[:, 384:512] + gnext[...].astype(F32)
    out_grad[...] = gown[...].astype(BF16)
    total = rin[0].astype(F32)
    for g in range(1, NX):
        total = total + rin[g].astype(F32)
    out_region[...] = total[:, 0:192].astype(BF16)

    for d in range(1, NZ):
        copy = remote(
            zout.at[z], zin.at[z], zas.at[d], zar.at[d], lax.rem(z + d, NZ) * NQ + q, x
        )
        copy.wait_recv()
        sent.append(copy)
    rows_a = mm(perm_a[...], zin[:, 0:32].reshape(512, 128)).astype(BF16)
    rows_b = mm(perm_b[...], zin[:, 32:48].reshape(256, 128)).astype(BF16)
    pout[:, 0:64] = rows_a.reshape(NQ, 64, 128)
    pout[:, 64:96] = rows_b.reshape(NQ, 32, 128)
    backs = []
    for d in range(1, NQ):
        to = lax.rem(q + d, NQ)
        backs.append(go(pout.at[to], pin.at[q], pbs.at[d], pbr.at[d], z * NQ + to, x))
    pin[q] = pout[q]
    for copy in backs:
        copy.wait_recv()
    for p in range(NQ):
        half = pin[p, 64:96].astype(F32)
        turned = pltpu.roll(half, 64, 1)
        for i in range(4):
            at = i * 128 + p * 16
            k = (i & 1) * 16
            rows_out[at : at + 16, 0:128] = pin[p, 16 * i : 16 * i + 16].astype(F32)
            rows_out[at : at + 16, 128:256] = (half if i < 2 else turned)[k : k + 16]
    for i in range(4):
        at = i * 128
        out_tile[0:128, at : at + 128] = jnp.transpose(rows_out[at : at + 128, 0:128]).astype(BF16)
        out_tile[128:192, at : at + 128] = jnp.transpose(rows_out[at : at + 128, 128:256])[
            0:64
        ].astype(BF16)
    for copy in sent:
        copy.wait_send()


def blocks_of(wide, out):
    for g in range(NX):
        at = g * 192 - (g & 1) * 64
        piece = wide[:, at : at + 256]
        out[g] = (pltpu.roll(piece, 192, 1) if g & 1 else piece).astype(BF16)


def finish(acopies, j, own_chunk, att, wrecv, wlast, zout, low64):
    for e in range(1, NX):
        acopies[e, j].wait_recv()
    chunk = lax.rem(own_chunk + j, 4)
    acc = jnp.zeros((128, 256), F32)
    upper = jnp.zeros((64, 256), F32)
    lower = jnp.zeros((64, 256), F32)
    for g in range(NX):
        acc = acc + mm(att[g, chunk, 0:128], wrecv[g, 0:128])
        upper = upper + mm(att[g, chunk, 128:192], wlast[g, 64:192])
        lower = lower + mm(att[g, chunk, 128:192], wlast[g, 0:128])
    acc = acc + jnp.concatenate([upper, lower], axis=0)
    two = acc[:, 128:256].reshape(4, 2, 16, 128)
    packed = jnp.where(
        low64,
        two[:, 0].reshape(64, 128),
        pltpu.roll(two[:, 1].reshape(64, 128), 64, 1),
    )
    at = chunk * 4
    zout[pl.ds(at, 4), 0:32] = acc[:, 0:128].reshape(4, 32, 128).astype(BF16)
    zout[pl.ds(at, 4), 32:48] = packed.reshape(4, 16, 128).astype(BF16)


def send_z(go, zout, zin, zas, zar, own_chunk, j, z, q, x):
    for k in range(4):
        to = lax.rem(own_chunk + j, 4) * 4 + k
        d = lax.rem(to - z + NZ, NZ)

        @pl.when(d != 0)
        def _():
            copy = pltpu.make_async_remote_copy(
                src_ref=zout.at[to],
                dst_ref=zin.at[z],
                send_sem=zas.at[d],
                recv_sem=zar.at[d],
                device_id={"seq": to * NQ + q, "head": x},
                device_id_type=MESH,
            )
            copy.start()


def body(
    tile_rows,
    tissue_mask,
    slide_lengths,
    region_rows,
    parent_lists,
    child_counts,
    region_cotangent,
    w_query,
    w_key,
    w_value,
    w_output,
    w_cross_query,
    w_cross_output,
):
    dma = pltpu.SemaphoreType.DMA
    vmem = lambda *shape: pltpu.VMEM(shape, BF16)
    tile_t, region, grad_t = pl.pallas_call(
        kernel,
        out_shape=(
            jax.ShapeDtypeStruct((192, 512), BF16),
            jax.ShapeDtypeStruct((32, 192), BF16),
            jax.ShapeDtypeStruct((192, 512), BF16),
        ),
        in_specs=[pl.BlockSpec(memory_space=pltpu.SMEM)]
        + [pl.BlockSpec(memory_space=pl.ANY)] * 2
        + [pl.BlockSpec(memory_space=pltpu.VMEM)] * 4
        + [pl.BlockSpec(memory_space=pl.ANY)] * 6,
        out_specs=(pl.BlockSpec(memory_space=pltpu.VMEM),) * 3,
        scratch_shapes=[
            vmem(512, 768),
            pltpu.VMEM((512, 128), jnp.int32),
            vmem(640, 768),
            vmem(192, 768),
            vmem(256, 768),
            vmem(192, 768),
            vmem(4, 192, 256),
            vmem(128, 768),
            vmem(16, 16, 384),
            vmem(16, 4, 16, 384),
            vmem(512, 640),
            vmem(768, 384),
            vmem(4, 192, 256),
            vmem(4, 192, 256),
            vmem(4, 4, 192, 128),
            vmem(16, 48, 128),
            vmem(16, 48, 128),
            vmem(8, 96, 128),
            vmem(8, 96, 128),
            vmem(2, 192, 128),
            pltpu.VMEM((192, 512), F32),
            vmem(192, 128),
            vmem(192, 128),
            vmem(4, 32, 256),
            vmem(4, 32, 256),
            vmem(512, 512),
            vmem(256, 256),
            pltpu.VMEM((512, 256), F32),
            dma((12,)),
            dma((8,)),
            dma((8,)),
            dma((16,)),
            dma((16,)),
            dma((4, 16)),
            dma((4, 16)),
            dma((4,)),
            dma((4,)),
            dma((2,)),
            dma((2,)),
            dma((4, 4)),
            dma((4, 4)),
            dma((16,)),
            dma((16,)),
            dma((8,)),
            dma((8,)),
            dma((2,)),
            dma((2,)),
            dma((4,)),
            dma((4,)),
        ],
        compiler_params=pltpu.CompilerParams(
            collective_id=0, has_side_effects=True, vmem_limit_bytes=60 * 1024 * 1024
        ),
    )(
        slide_lengths,
        tile_rows,
        tissue_mask.reshape(512, 128),
        region_rows,
        parent_lists.T,
        child_counts.reshape(1, 32),
        region_cotangent,
        w_query.T,
        w_key.T,
        w_value.T,
        w_output,
        w_cross_query.T,
        w_cross_output,
    )
    return tile_t.T, region, grad_t.T


def solution(mesh):
    in_specs = (
        P("seq", None),
        P(),
        P(),
        P("seq", None),
        P("seq", None),
        P("seq"),
        P("seq", None),
        P(None, "head"),
        P(None, "head"),
        P(None, "head"),
        P("head", None),
        P(None, "head"),
        P("head", None),
    )
    out_specs = (P("seq", "head"), P("seq", "head"), P("seq", "head"))
    return jax.shard_map(body, mesh=mesh, in_specs=in_specs, out_specs=out_specs, check_vma=False)
```

```python
import functools

import jax
import jax.numpy as jnp
from jax import lax
from jax.experimental import pallas as pl
from jax.experimental.pallas import tpu as pltpu
from jax.sharding import PartitionSpec as P

HD = 64
NZ = 16
NQ = 8
NX = 4
MESH = pl.DeviceIdType.MESH
F32 = jnp.float32
BF16 = jnp.bfloat16
NEG = -1e30
ZORDER = (1, 15, 2, 14, 3, 13, 4, 12, 5, 11, 6, 10, 7, 9, 8)


def iota(shape, dim):
    return lax.broadcasted_iota(jnp.int32, shape, dim)


def nt(a, b):
    return lax.dot_general(a, b, (((1,), (1,)), ((), ())), preferred_element_type=F32)


def tn(a, b):
    return lax.dot_general(a, b, (((0,), (0,)), ((), ())), preferred_element_type=F32)


def mm(a, b):
    return jnp.dot(a, b, preferred_element_type=F32)


def order_of(row):
    return (row & ~31) | ((row & 7) << 2) | ((row >> 3) & 3)


def kernel(
    lengths,
    tiles,
    tissue,
    regions,
    parents,
    counts,
    cotangent,
    wq_t,
    wk_t,
    wv_t,
    wo,
    wcq_t,
    wco,
    out_tile,
    out_region,
    out_grad,
    tiles_in,
    tissue_in,
    regions_in,
    parents_in,
    counts_in,
    cot_in,
    lens,
    w_t,
    wo_in,
    wcq_in,
    wco_in,
    wout,
    first,
    second,
    feats,
    qkv,
    ext,
    wrecv,
    wlast,
    att,
    zout,
    zin,
    pout,
    pin,
    gext,
    gown,
    gprev,
    gnext,
    rout,
    rin,
    perm_a,
    perm_b,
    rows_out,
    loads,
    p1s,
    p1r,
    p2s,
    p2r,
    pxs,
    pxr,
    wos,
    wor,
    has,
    har,
    axs,
    axr,
    zas,
    zar,
    pbs,
    pbr,
    grs,
    grr,
    res,
    rer,
):
    s = lax.axis_index("seq")
    x = lax.axis_index("head")
    z = s // NQ
    q = lax.rem(s, NQ)
    n_seq = NZ * NQ
    after = lax.rem(s + 1, n_seq)
    before = lax.rem(s + n_seq - 1, n_seq)

    def remote(src, dst, ss, rs, seq, head):
        return pltpu.make_async_remote_copy(
            src_ref=src,
            dst_ref=dst,
            send_sem=ss,
            recv_sem=rs,
            device_id={"seq": seq, "head": head},
            device_id_type=MESH,
        )

    sent = []

    def go(*args):
        copy = remote(*args)
        copy.start()
        sent.append(copy)
        return copy

    barrier = pltpu.get_barrier_semaphore()

    def greet(seq, head):
        pl.semaphore_signal(
            barrier, inc=1, device_id={"seq": seq, "head": head}, device_id_type=MESH
        )

    for d in range(1, NQ):
        greet(z * NQ + lax.rem(q + d, NQ), x)
    for d in ZORDER:
        greet(lax.rem(z + d, NZ) * NQ + q, x)
    for d in range(1, NX):
        greet(s, lax.rem(x + d, NX))
    greet(after, x)
    greet(before, x)
    pl.semaphore_wait(barrier, (NQ - 1) + (NZ - 1) + (NX - 1) + 2)

    hop1 = []
    for d in range(1, NQ):
        to = lax.rem(q + d, NQ)
        hop1.append(
            go(
                tiles.at[pl.ds(pl.multiple_of(x * 128 + to * 16, 16), 16)],
                first.at[pl.ds(pl.multiple_of(q * 16, 16), 16)],
                p1s.at[d],
                p1r.at[d],
                z * NQ + to,
                x,
            )
        )
    local = []

    def load(src, dst):
        copy = pltpu.make_async_copy(src, dst, loads.at[len(local)])
        copy.start()
        local.append(copy)
        return copy

    load_tiles = load(tiles, tiles_in)
    load_w = [
        load(wk_t.at[0:128], w_t.at[128:256]),
        load(wv_t.at[0:128], w_t.at[256:384]),
        load(wk_t.at[128:192], w_t.at[512:576]),
        load(wv_t.at[128:192], w_t.at[576:640]),
        load(wq_t.at[0:128], w_t.at[0:128]),
        load(wq_t.at[128:192], w_t.at[384:448]),
    ]
    load_wo = load(wo, wo_in)
    load_wcq = load(wcq_t, wcq_in.at[0:192])
    load_wco = load(wco, wco_in)
    load_regions = [
        load(regions, regions_in),
        load(parents, parents_in),
        load(counts, counts_in),
        load(cotangent, cot_in),
    ]
    load_mask = [load(tissue, tissue_in), load(lengths, lens)]


    load_wo.wait()
    blocks_of(wo_in[...].astype(F32), wout)
    wcopies = []
    for d in range(1, NX):
        to = lax.rem(x + d, NX)
        wcopies.append(go(wout.at[to], wrecv.at[x], wos.at[d], wor.at[d], s, to))
    wrecv[x] = wout[x]

    load_tiles.wait()
    for copy in load_w:
        copy.wait()
    w_t[448:512] = jnp.zeros((64, 768), BF16)
    first[pl.ds(pl.multiple_of(q * 16, 16), 16), :] = tiles_in[
        pl.ds(pl.multiple_of(x * 128 + q * 16, 16), 16), :
    ]
    block = tiles_in[...]
    ext[128:640, 0:256] = nt(block, w_t[128:384]).astype(BF16)
    ext[128:640, 256:384] = nt(block, w_t[512:640]).astype(BF16)
    halos = [
        go(ext.at[128:256], ext.at[640:768], has.at[0], har.at[0], before, x),
        go(ext.at[512:640], ext.at[0:128], has.at[1], har.at[1], after, x),
    ]

    lane = iota((256, 128), 1)
    row = iota((256, 128), 0)
    source = (lane & 15) * 16 + (lane >> 4)
    turn0 = (source == row).astype(BF16)
    turn1 = (source + 8 == row).astype(BF16)
    for copy in hop1:
        copy.wait_recv()
    second[...] = (
        (mm(turn0, first[:, 0:384]) + mm(turn1, first[:, 384:768]))
        .astype(BF16)
        .reshape(NZ, 16, 384)
    )
    hop2 = {}
    for d in ZORDER:
        to = lax.rem(z + d, NZ)
        hop2[d] = go(second.at[to], feats.at[z, x], p2s.at[d], p2r.at[d], to * NQ + q, x)
    feats[z, x] = second[z]

    right = lax.rem(x + 1, NX)
    left = lax.rem(x + 3, NX)
    hopx = {}
    steps = (0,) + ZORDER

    def place_of(k):
        return lax.rem(z - steps[k] + NZ, NZ)

    def spread(k):
        at = place_of(k)
        part = feats.at[at, x]
        hopx[0, k] = go(part, part, pxs.at[0, k], pxr.at[0, k], s, right)
        hopx[1, k] = go(part, part, pxs.at[1, k], pxr.at[1, k], s, left)

    def relay(k):
        hopx.pop((k % 2, k)).wait_recv()
        part = feats.at[place_of(k), right if k % 2 else left]
        hopx[2, k] = go(part, part, pxs.at[2, k], pxr.at[2, k], s, left if k % 2 else right)

    def arrive(k):
        hop2[steps[k]].wait_recv()
        spread(k)
        if k >= 2:
            relay(k - 2)

    spread(0)

    low = iota((32, 128), 1) < HD
    load_wcq.wait()
    load_wco.wait()
    for copy in load_regions:
        copy.wait()
    rows32 = regions_in[...]
    wcq_in[192:256] = jnp.zeros((64, 768), BF16)
    cq = nt(rows32, wcq_in[...]).astype(BF16).astype(F32) * (HD**-0.5)
    rk = nt(rows32, w_t[128:384]).astype(BF16).astype(F32)
    rkv2 = nt(rows32, w_t[512:640]).astype(BF16).astype(F32)
    rk01, rv01 = rk[:, 0:128], rk[:, 128:256]
    cq0 = jnp.where(low, cq[:, 0:128], 0.0)
    cq1 = jnp.where(low, 0.0, cq[:, 0:128])
    cq2 = jnp.where(low, cq[:, 128:256], 0.0)
    back_t = nt(wco_in[...], cot_in[...]).astype(BF16)
    place = iota((32, 768), 1)
    times = jnp.zeros((32, 768), F32)
    base = s * 512 - 128
    lists = jnp.where(iota((16, 32), 0) < counts_in[...], parents_in[...] - base, -1)
    lists = jnp.transpose(lists.astype(F32)).astype(jnp.int32)
    for j in range(16):
        times = times + jnp.where(lists[:, j : j + 1] == place, 1.0, 0.0)
    valid = times > 0.0
    for copy in halos:
        copy.wait_recv()
    outs = []
    for h in range(3):
        query = (cq0, cq1, cq2)[h]
        own = jnp.sum(query * (rk01 if h < 2 else rkv2), axis=1, keepdims=True)
        keys = ext[:, 0:128] if h < 2 else ext[:, 256:384]
        values = ext[:, 128:256] if h < 2 else keys
        sc = jnp.where(valid, nt(query.astype(BF16), keys), NEG)
        top = jnp.maximum(own, jnp.max(sc, axis=1, keepdims=True))
        ex = jnp.where(valid, jnp.exp(sc - top), 0.0)
        ex_own = jnp.exp(own - top)
        total = ex_own + jnp.sum(times * ex, axis=1, keepdims=True)
        weight = (ex / total).astype(BF16).astype(F32)
        weight_own = (ex_own / total).astype(BF16).astype(F32)
        mixed = (times * weight).astype(BF16)
        outs.append(mm(mixed, values) + weight_own * (rv01 if h < 2 else rkv2))
        grad = mm(back_t[64 * h : 64 * h + 64], mixed)
        gown[64 * h : 64 * h + 64] = grad[:, 128:640]
        gext[0, 64 * h : 64 * h + 64] = grad[:, 0:128].astype(BF16)
        gext[1, 64 * h : 64 * h + 64] = grad[:, 640:768].astype(BF16)
    cross_a = jnp.where(low, outs[0], outs[1]).astype(BF16)
    cross_b = pltpu.roll(outs[2], 64, 1)[:, 0:64].astype(BF16)
    gcopies = [
        go(gext.at[0], gnext, grs.at[0], grr.at[0], before, x),
        go(gext.at[1], gprev, grs.at[1], grr.at[1], after, x),
    ]
    blocks_of(mm(cross_a, wco_in[0:128]) + mm(cross_b, wco_in[128:192]), rout)
    rcopies = []
    for d in range(1, NX):
        to = lax.rem(x + d, NX)
        rcopies.append(go(rout.at[to], rin.at[x], res.at[d], rer.at[d], s, to))
    rin[x] = rout[x]

    for k in range(1, 8):
        arrive(k)

    prow = iota((512, 512), 0)
    pcol = iota((512, 512), 1)
    perm_a[...] = (
        ((prow & 15) * 32 + ((prow >> 4) & 3) * 8 + (prow >> 6)) == pcol
    ).astype(BF16)
    prow = iota((256, 256), 0)
    pcol = iota((256, 256), 1)
    perm_b[...] = (
        ((prow & 15) * 16 + ((prow >> 4) & 1) * 8 + (prow >> 5)) == pcol
    ).astype(BF16)
    wlast[:, 0:64] = jnp.zeros((NX, 64, 256), BF16)
    wlast[:, 128:192] = jnp.zeros((NX, 64, 256), BF16)

    c = q * NZ + z
    for copy in load_mask:
        copy.wait()
    pick = (iota((16, 128), 1) == c).astype(BF16)
    tissue_n = nt(pick, tissue_in[...].astype(F32).astype(BF16)).astype(BF16)
    spread_n = (iota((512, 512), 0) == order_of(iota((512, 512), 1))).astype(BF16)
    tissue_row = mm(tissue_n, spread_n)[0:1]
    n_row = order_of(iota((1, 512), 1))
    slide_row = jnp.zeros((1, 512), jnp.int32)
    end = jnp.int32(0)
    for k in range(8):
        end = end + lens[k]
        slide_row = slide_row + jnp.where(n_row * 128 + c >= end, 1, 0)

    for k in range(8, 16):
        arrive(k)
    relay(14)
    relay(15)
    w_out_rows(wcopies, wrecv, wlast)

    for b in range(4):
        group = range(4 * b, 4 * b + 4)
        for k in group:
            for e in range(3):
                if (e, k) in hopx:
                    hopx[e, k].wait_recv()
        part = jnp.stack([feats[place_of(k)] for k in group]).astype(F32)
        part = part.reshape(16, 2, 8, 384)
        upper = part[:, 0].reshape(128, 384).astype(BF16)
        lower = part[:, 1].reshape(128, 384).astype(BF16)
        made = nt(upper, w_t[:, 0:384]) + nt(lower, w_t[:, 384:768])
        made = made.astype(BF16).reshape(4, 32, 640)
        for i in range(4):
            qkv[place_of(group[i])] = made[i]
    every = qkv[...].reshape(512, 640)

    low128 = iota((128, 128), 1) < HD
    keys01 = every[:, 128:256].astype(F32)
    low512 = iota((512, 128), 1) < HD
    key0 = jnp.where(low512, keys01, 0.0).astype(BF16)
    key1 = jnp.where(low512, 0.0, keys01).astype(BF16)
    key_value2 = every[:, 512:640]
    values01 = every[:, 256:384]
    has_tissue = tissue_row > 0.5
    own_chunk = z // 4
    low64 = iota((64, 128), 1) < HD

    acopies = {}
    zcopies = []
    chunks = [lax.rem(own_chunk + k, 4) for k in (2, 1, 3, 0)]

    def pass_on(j):
        acopies.pop((0, j)).wait_recv()
        part = att.at[left, chunks[j], 0:96]
        acopies[2, j] = go(part, part, axs.at[2, j], axr.at[2, j], s, right)
        acopies.pop((1, j)).wait_recv()
        part = att.at[right, chunks[j], 96:192]
        acopies[3, j] = go(part, part, axs.at[3, j], axr.at[3, j], s, left)

    def finish(j):
        acopies[2, j].wait_recv()
        acopies[3, j].wait_recv()
        output_rows(chunks[j], att, wrecv, wlast, zout, low64)
        for k in range(4):
            if (j, k) != (3, 0):
                to = chunks[j] * 4 + lax.rem(z + k, 4)
                zcopies.append(
                    go(zout.at[to], zin.at[z], zas.at[j, k], zar.at[j, k], to * NQ + q, x)
                )

    for j in range(4):
        chunk = chunks[j]
        at = pl.multiple_of(chunk * 128, 128)
        query = qkv[pl.ds(chunk * 4, 4)].reshape(128, 640)
        query01 = (query[:, 0:128].astype(F32) * (HD**-0.5)).astype(BF16)
        query2 = (query[:, 384:512].astype(F32) * (HD**-0.5)).astype(BF16)
        row = iota((128, 1), 0) + at
        n_mine = order_of(row)
        slide_mine = jnp.zeros((128, 1), jnp.int32)
        end = jnp.int32(0)
        for k in range(8):
            end = end + lens[k]
            slide_mine = slide_mine + jnp.where(n_mine * 128 + c >= end, 1, 0)
        base_ok = (slide_mine == slide_row) & (has_tissue | (row == iota((128, 512), 1)))
        parts = []
        for h in range(3):
            step = (jnp.int32(1) << lax.rem(3 * x + h, 4)) - 1
            allowed = base_ok & ((n_mine & step) == (n_row & step))
            sc = nt(query01 if h < 2 else query2, (key0, key1, key_value2)[h])
            sc = jnp.where(allowed, sc, NEG)
            ex = jnp.exp(sc - jnp.max(sc, axis=1, keepdims=True))
            total = jnp.sum(ex, axis=1, keepdims=True)
            parts.append(mm(ex.astype(BF16), values01 if h < 2 else key_value2) / total)
        att[x, chunk, 0:128] = jnp.where(low128, parts[0], parts[1]).astype(BF16)
        att[x, chunk, 128:192] = jnp.where(
            low64, pltpu.roll(parts[2][0:64], 64, 1), parts[2][64:128]
        ).astype(BF16)
        part = att.at[x, chunk]
        acopies[0, j] = go(part, part, axs.at[0, j], axr.at[0, j], s, right)
        acopies[1, j] = go(part, part, axs.at[1, j], axr.at[1, j], s, left)
        if j >= 1:
            pass_on(j - 1)
        if j >= 2:
            finish(j - 2)
    pass_on(3)
    finish(2)
    finish(3)
    zin[z] = zout[z]

    for copy in gcopies + rcopies:
        copy.wait_recv()
    gown[:, 0:128] = gown[:, 0:128] + gprev[...].astype(F32)
    gown[:, 384:512] = gown[:, 384:512] + gnext[...].astype(F32)
    out_grad[...] = gown[...].astype(BF16)
    total = rin[0].astype(F32)
    for g in range(1, NX):
        total = total + rin[g].astype(F32)
    out_region[...] = total[:, 0:192].astype(BF16)

    for copy in zcopies:
        copy.wait_recv()
    rows_a = mm(perm_a[...], zin[:, 0:32].reshape(512, 128)).astype(BF16)
    rows_b = mm(perm_b[...], zin[:, 32:48].reshape(256, 128)).astype(BF16)
    pout[:, 0:64] = rows_a.reshape(NQ, 64, 128)
    pout[:, 64:96] = rows_b.reshape(NQ, 32, 128)
    backs = []
    for d in range(1, NQ):
        to = lax.rem(q + d, NQ)
        backs.append(go(pout.at[to], pin.at[q], pbs.at[d], pbr.at[d], z * NQ + to, x))
    pin[q] = pout[q]
    for copy in backs:
        copy.wait_recv()
    for p in range(NQ):
        half = pin[p, 64:96].astype(F32)
        turned = pltpu.roll(half, 64, 1)
        for i in range(4):
            at = i * 128 + p * 16
            k = (i & 1) * 16
            rows_out[at : at + 16, 0:128] = pin[p, 16 * i : 16 * i + 16].astype(F32)
            rows_out[at : at + 16, 128:256] = (half if i < 2 else turned)[k : k + 16]
    for i in range(4):
        at = i * 128
        out_tile[0:128, at : at + 128] = jnp.transpose(rows_out[at : at + 128, 0:128]).astype(BF16)
        out_tile[128:192, at : at + 128] = jnp.transpose(rows_out[at : at + 128, 128:256])[
            0:64
        ].astype(BF16)
    for copy in sent:
        copy.wait_send()


def blocks_of(wide, out):
    for g in range(NX):
        at = g * 192 - (g & 1) * 64
        piece = wide[:, at : at + 256]
        out[g] = (pltpu.roll(piece, 192, 1) if g & 1 else piece).astype(BF16)


def w_out_rows(wcopies, wrecv, wlast):
    for copy in wcopies:
        copy.wait_recv()
    wlast[:, 64:128] = wrecv[:, 128:192]


def output_rows(chunk, att, wrecv, wlast, zout, low64):
    acc = jnp.zeros((128, 256), F32)
    upper = jnp.zeros((64, 256), F32)
    lower = jnp.zeros((64, 256), F32)
    for g in range(NX):
        acc = acc + mm(att[g, chunk, 0:128], wrecv[g, 0:128])
        upper = upper + mm(att[g, chunk, 128:192], wlast[g, 64:192])
        lower = lower + mm(att[g, chunk, 128:192], wlast[g, 0:128])
    acc = acc + jnp.concatenate([upper, lower], axis=0)
    two = acc[:, 128:256].reshape(4, 2, 16, 128)
    packed = jnp.where(
        low64,
        two[:, 0].reshape(64, 128),
        pltpu.roll(two[:, 1].reshape(64, 128), 64, 1),
    )
    at = chunk * 4
    zout[pl.ds(at, 4), 0:32] = acc[:, 0:128].reshape(4, 32, 128).astype(BF16)
    zout[pl.ds(at, 4), 32:48] = packed.reshape(4, 16, 128).astype(BF16)


def body(
    tile_rows,
    tissue_mask,
    slide_lengths,
    region_rows,
    parent_lists,
    child_counts,
    region_cotangent,
    w_query,
    w_key,
    w_value,
    w_output,
    w_cross_query,
    w_cross_output,
):
    dma = pltpu.SemaphoreType.DMA
    vmem = lambda *shape: pltpu.VMEM(shape, BF16)
    tile_t, region, grad_t = pl.pallas_call(
        kernel,
        out_shape=(
            jax.ShapeDtypeStruct((192, 512), BF16),
            jax.ShapeDtypeStruct((32, 192), BF16),
            jax.ShapeDtypeStruct((192, 512), BF16),
        ),
        in_specs=[pl.BlockSpec(memory_space=pl.ANY)] * 13,
        out_specs=(pl.BlockSpec(memory_space=pltpu.VMEM),) * 3,
        scratch_shapes=[
            vmem(512, 768),
            pltpu.VMEM((512, 128), jnp.int32),
            vmem(32, 768),
            pltpu.VMEM((16, 32), jnp.int32),
            pltpu.VMEM((1, 32), jnp.int32),
            vmem(32, 768),
            pltpu.SMEM((8,), jnp.int32),
            vmem(640, 768),
            vmem(192, 768),
            vmem(256, 768),
            vmem(192, 768),
            vmem(4, 192, 256),
            vmem(128, 768),
            vmem(16, 16, 384),
            vmem(16, 4, 16, 384),
            vmem(16, 32, 640),
            vmem(768, 384),
            vmem(4, 192, 256),
            vmem(4, 192, 256),
            vmem(4, 4, 192, 128),
            vmem(16, 48, 128),
            vmem(16, 48, 128),
            vmem(8, 96, 128),
            vmem(8, 96, 128),
            vmem(2, 192, 128),
            pltpu.VMEM((192, 512), F32),
            vmem(192, 128),
            vmem(192, 128),
            vmem(4, 32, 256),
            vmem(4, 32, 256),
            vmem(512, 512),
            vmem(256, 256),
            pltpu.VMEM((512, 256), F32),
            dma((16,)),
            dma((8,)),
            dma((8,)),
            dma((16,)),
            dma((16,)),
            dma((4, 16)),
            dma((4, 16)),
            dma((4,)),
            dma((4,)),
            dma((2,)),
            dma((2,)),
            dma((4, 4)),
            dma((4, 4)),
            dma((4, 4)),
            dma((4, 4)),
            dma((8,)),
            dma((8,)),
            dma((2,)),
            dma((2,)),
            dma((4,)),
            dma((4,)),
        ],
        compiler_params=pltpu.CompilerParams(
            collective_id=0, has_side_effects=True, vmem_limit_bytes=60 * 1024 * 1024
        ),
    )(
        slide_lengths,
        tile_rows,
        tissue_mask.reshape(512, 128),
        region_rows,
        parent_lists.T,
        child_counts.reshape(1, 32),
        region_cotangent,
        w_query.T,
        w_key.T,
        w_value.T,
        w_output,
        w_cross_query.T,
        w_cross_output,
    )
    return tile_t.T, region, grad_t.T


def solution(mesh):
    in_specs = (
        P("seq", None),
        P(),
        P(),
        P("seq", None),
        P("seq", None),
        P("seq"),
        P("seq", None),
        P(None, "head"),
        P(None, "head"),
        P(None, "head"),
        P("head", None),
        P(None, "head"),
        P("head", None),
    )
    out_specs = (P("seq", "head"), P("seq", "head"), P("seq", "head"))
    return jax.shard_map(body, mesh=mesh, in_specs=in_specs, out_specs=out_specs, check_vma=False)
```

```python
import functools

import jax
import jax.numpy as jnp
from jax import lax
from jax.experimental import pallas as pl
from jax.experimental.pallas import tpu as pltpu
from jax.sharding import PartitionSpec as P

HD = 64
NZ = 16
NQ = 8
NX = 4
MESH = pl.DeviceIdType.MESH
F32 = jnp.float32
BF16 = jnp.bfloat16
NEG = -1e30
ZORDER = (1, 15, 2, 14, 3, 13, 4, 12, 5, 11, 6, 10, 7, 9, 8)


def iota(shape, dim):
    return lax.broadcasted_iota(jnp.int32, shape, dim)


def nt(a, b):
    return lax.dot_general(a, b, (((1,), (1,)), ((), ())), preferred_element_type=F32)


def tn(a, b):
    return lax.dot_general(a, b, (((0,), (0,)), ((), ())), preferred_element_type=F32)


def mm(a, b):
    return jnp.dot(a, b, preferred_element_type=F32)


def order_of(row, z):
    k = row >> 5
    near = (k + 1) >> 1
    zk = (z + jnp.where((k & 1) == 1, -near, near)) & (NZ - 1)
    return (zk << 5) | ((row & 7) << 2) | ((row >> 3) & 3)


def kernel(
    lengths,
    tiles,
    tissue,
    regions,
    parents,
    counts,
    cotangent,
    wq_t,
    wk_t,
    wv_t,
    wo,
    wcq_t,
    wco,
    out_tile,
    out_region,
    out_grad,
    tiles_in,
    tissue_in,
    regions_in,
    parents_in,
    counts_in,
    cot_in,
    lens,
    w_t,
    wo_in,
    wcq_in,
    wco_in,
    wout,
    first,
    second,
    feats,
    qkv,
    ext,
    wrecv,
    wlast,
    att,
    zout,
    zin,
    pout,
    pin,
    gext,
    gown,
    gprev,
    gnext,
    rout,
    rin,
    perm_a,
    perm_b,
    rows_out,
    loads,
    p1s,
    p1r,
    p2s,
    p2r,
    pxs,
    pxr,
    wos,
    wor,
    has,
    har,
    axs,
    axr,
    zas,
    zar,
    pbs,
    pbr,
    grs,
    grr,
    res,
    rer,
):
    s = lax.axis_index("seq")
    x = lax.axis_index("head")
    z = s // NQ
    q = lax.rem(s, NQ)
    n_seq = NZ * NQ
    after = lax.rem(s + 1, n_seq)
    before = lax.rem(s + n_seq - 1, n_seq)

    def remote(src, dst, ss, rs, seq, head):
        return pltpu.make_async_remote_copy(
            src_ref=src,
            dst_ref=dst,
            send_sem=ss,
            recv_sem=rs,
            device_id={"seq": seq, "head": head},
            device_id_type=MESH,
        )

    sent = []

    def go(*args):
        copy = remote(*args)
        copy.start()
        sent.append(copy)
        return copy

    barrier = pltpu.get_barrier_semaphore()

    def greet(seq, head):
        pl.semaphore_signal(
            barrier, inc=1, device_id={"seq": seq, "head": head}, device_id_type=MESH
        )

    for d in range(1, NQ):
        greet(z * NQ + lax.rem(q + d, NQ), x)
    for d in ZORDER:
        greet(lax.rem(z + d, NZ) * NQ + q, x)
    for d in range(1, NX):
        greet(s, lax.rem(x + d, NX))
    greet(after, x)
    greet(before, x)
    pl.semaphore_wait(barrier, (NQ - 1) + (NZ - 1) + (NX - 1) + 2)

    hop1 = []
    for d in range(1, NQ):
        to = lax.rem(q + d, NQ)
        hop1.append(
            go(
                tiles.at[pl.ds(pl.multiple_of(x * 128 + to * 16, 16), 16)],
                first.at[pl.ds(pl.multiple_of(q * 16, 16), 16)],
                p1s.at[d],
                p1r.at[d],
                z * NQ + to,
                x,
            )
        )
    local = []

    def load(src, dst):
        copy = pltpu.make_async_copy(src, dst, loads.at[len(local)])
        copy.start()
        local.append(copy)
        return copy

    load_tiles = load(tiles, tiles_in)
    load_w = [
        load(wk_t.at[0:128], w_t.at[128:256]),
        load(wv_t.at[0:128], w_t.at[256:384]),
        load(wk_t.at[128:192], w_t.at[512:576]),
        load(wv_t.at[128:192], w_t.at[576:640]),
        load(wq_t.at[0:128], w_t.at[0:128]),
        load(wq_t.at[128:192], w_t.at[384:448]),
    ]
    load_wo = load(wo, wo_in)
    load_wcq = load(wcq_t, wcq_in.at[0:192])
    load_wco = load(wco, wco_in)
    load_regions = [
        load(regions, regions_in),
        load(parents, parents_in),
        load(counts, counts_in),
        load(cotangent, cot_in),
    ]
    load_mask = [load(tissue, tissue_in), load(lengths, lens)]


    load_wo.wait()
    blocks_of(wo_in[...].astype(F32), wout)
    wcopies = []
    for d in range(1, NX):
        to = lax.rem(x + d, NX)
        wcopies.append(go(wout.at[to], wrecv.at[x], wos.at[d], wor.at[d], s, to))
    wrecv[x] = wout[x]

    load_tiles.wait()
    for copy in load_w:
        copy.wait()
    w_t[448:512] = jnp.zeros((64, 768), BF16)
    first[pl.ds(pl.multiple_of(q * 16, 16), 16), :] = tiles_in[
        pl.ds(pl.multiple_of(x * 128 + q * 16, 16), 16), :
    ]
    block = tiles_in[...]
    ext[128:640, 0:256] = nt(block, w_t[128:384]).astype(BF16)
    ext[128:640, 256:384] = nt(block, w_t[512:640]).astype(BF16)
    halos = [
        go(ext.at[128:256], ext.at[640:768], has.at[0], har.at[0], before, x),
        go(ext.at[512:640], ext.at[0:128], has.at[1], har.at[1], after, x),
    ]

    lane = iota((256, 128), 1)
    row = iota((256, 128), 0)
    source = (lane & 15) * 16 + (lane >> 4)
    turn0 = (source == row).astype(BF16)
    turn1 = (source + 8 == row).astype(BF16)
    for copy in hop1:
        copy.wait_recv()
    second[...] = (
        (mm(turn0, first[:, 0:384]) + mm(turn1, first[:, 384:768]))
        .astype(BF16)
        .reshape(NZ, 16, 384)
    )
    steps = (0,) + ZORDER
    hop2 = {}
    for k in range(1, NZ):
        to = lax.rem(z + steps[k], NZ)
        hop2[k] = go(second.at[to], feats.at[x, k], p2s.at[k], p2r.at[k], to * NQ + q, x)
    feats[x, 0] = second[z]

    right = lax.rem(x + 1, NX)
    left = lax.rem(x + 3, NX)
    hopx = {}

    def spread(b):
        for k in range(4 * b, 4 * b + 4):
            if k:
                hop2[k].wait_recv()
        part = feats.at[x, 4 * b : 4 * b + 4]
        hopx[0, b] = go(part, part, pxs.at[0, b], pxr.at[0, b], s, right)
        hopx[1, b] = go(part, part, pxs.at[1, b], pxr.at[1, b], s, left)

    def relay(b):
        hopx[0, b].wait_recv()
        part = feats.at[left, 4 * b : 4 * b + 2]
        hopx[2, b] = go(part, part, pxs.at[2, b], pxr.at[2, b], s, right)
        hopx[1, b].wait_recv()
        part = feats.at[right, 4 * b + 2 : 4 * b + 4]
        hopx[3, b] = go(part, part, pxs.at[3, b], pxr.at[3, b], s, left)

    def project(b):
        hopx[2, b].wait_recv()
        hopx[3, b].wait_recv()
        part = [feats[i, k].astype(F32) for k in range(4 * b, 4 * b + 4) for i in range(NX)]
        upper = jnp.concatenate([p[0:8] for p in part], axis=0).astype(BF16)
        lower = jnp.concatenate([p[8:16] for p in part], axis=0).astype(BF16)
        qkv[128 * b : 128 * b + 128] = (
            nt(upper, w_t[:, 0:384]) + nt(lower, w_t[:, 384:768])
        ).astype(BF16)

    low = iota((32, 128), 1) < HD
    load_wcq.wait()
    load_wco.wait()
    for copy in load_regions:
        copy.wait()
    rows32 = regions_in[...]
    wcq_in[192:256] = jnp.zeros((64, 768), BF16)
    cq = nt(rows32, wcq_in[...]).astype(BF16).astype(F32) * (HD**-0.5)
    rk = nt(rows32, w_t[128:384]).astype(BF16).astype(F32)
    rkv2 = nt(rows32, w_t[512:640]).astype(BF16).astype(F32)
    rk01, rv01 = rk[:, 0:128], rk[:, 128:256]
    cq0 = jnp.where(low, cq[:, 0:128], 0.0)
    cq1 = jnp.where(low, 0.0, cq[:, 0:128])
    cq2 = jnp.where(low, cq[:, 128:256], 0.0)
    back_t = nt(wco_in[...], cot_in[...]).astype(BF16)
    place = iota((32, 768), 1)
    times = jnp.zeros((32, 768), F32)
    base = s * 512 - 128
    lists = jnp.where(iota((16, 32), 0) < counts_in[...], parents_in[...] - base, -1)
    lists = jnp.transpose(lists.astype(F32)).astype(jnp.int32)
    for j in range(16):
        times = times + jnp.where(lists[:, j : j + 1] == place, 1.0, 0.0)
    valid = times > 0.0
    for copy in halos:
        copy.wait_recv()
    outs = []
    for h in range(3):
        query = (cq0, cq1, cq2)[h]
        own = jnp.sum(query * (rk01 if h < 2 else rkv2), axis=1, keepdims=True)
        keys = ext[:, 0:128] if h < 2 else ext[:, 256:384]
        values = ext[:, 128:256] if h < 2 else keys
        sc = jnp.where(valid, nt(query.astype(BF16), keys), NEG)
        top = jnp.maximum(own, jnp.max(sc, axis=1, keepdims=True))
        ex = jnp.where(valid, jnp.exp(sc - top), 0.0)
        ex_own = jnp.exp(own - top)
        total = ex_own + jnp.sum(times * ex, axis=1, keepdims=True)
        weight = (ex / total).astype(BF16).astype(F32)
        weight_own = (ex_own / total).astype(BF16).astype(F32)
        mixed = (times * weight).astype(BF16)
        outs.append(mm(mixed, values) + weight_own * (rv01 if h < 2 else rkv2))
        grad = mm(back_t[64 * h : 64 * h + 64], mixed)
        gown[64 * h : 64 * h + 64] = grad[:, 128:640]
        gext[0, 64 * h : 64 * h + 64] = grad[:, 0:128].astype(BF16)
        gext[1, 64 * h : 64 * h + 64] = grad[:, 640:768].astype(BF16)
    cross_a = jnp.where(low, outs[0], outs[1]).astype(BF16)
    cross_b = pltpu.roll(outs[2], 64, 1)[:, 0:64].astype(BF16)
    gcopies = [
        go(gext.at[0], gnext, grs.at[0], grr.at[0], before, x),
        go(gext.at[1], gprev, grs.at[1], grr.at[1], after, x),
    ]
    blocks_of(mm(cross_a, wco_in[0:128]) + mm(cross_b, wco_in[128:192]), rout)
    rcopies = []
    for d in range(1, NX):
        to = lax.rem(x + d, NX)
        rcopies.append(go(rout.at[to], rin.at[x], res.at[d], rer.at[d], s, to))
    rin[x] = rout[x]

    spread(0)

    prow = iota((512, 512), 0)
    pcol = iota((512, 512), 1)
    perm_a[...] = (
        ((prow & 15) * 32 + ((prow >> 4) & 3) * 8 + (prow >> 6)) == pcol
    ).astype(BF16)
    prow = iota((256, 256), 0)
    pcol = iota((256, 256), 1)
    perm_b[...] = (
        ((prow & 15) * 16 + ((prow >> 4) & 1) * 8 + (prow >> 5)) == pcol
    ).astype(BF16)
    wlast[:, 0:64] = jnp.zeros((NX, 64, 256), BF16)
    wlast[:, 128:192] = jnp.zeros((NX, 64, 256), BF16)

    c = q * NZ + z
    for copy in load_mask:
        copy.wait()
    pick = (iota((16, 128), 1) == c).astype(BF16)
    tissue_n = nt(pick, tissue_in[...].astype(F32).astype(BF16)).astype(BF16)
    spread_n = (iota((512, 512), 0) == order_of(iota((512, 512), 1), z)).astype(BF16)
    tissue_row = mm(tissue_n, spread_n)[0:1]
    n_row = order_of(iota((1, 512), 1), z)
    slide_row = jnp.zeros((1, 512), jnp.int32)
    end = jnp.int32(0)
    for k in range(8):
        end = end + lens[k]
        slide_row = slide_row + jnp.where(n_row * 128 + c >= end, 1, 0)

    spread(1)
    relay(0)
    w_out_rows(wcopies, wrecv, wlast)
    spread(2)
    relay(1)
    project(0)
    spread(3)
    relay(2)
    project(1)
    relay(3)
    project(2)
    project(3)
    every = qkv[...]

    low128 = iota((128, 128), 1) < HD
    keys01 = every[:, 128:256].astype(F32)
    low512 = iota((512, 128), 1) < HD
    key0 = jnp.where(low512, keys01, 0.0).astype(BF16)
    key1 = jnp.where(low512, 0.0, keys01).astype(BF16)
    key_value2 = every[:, 512:640]
    values01 = every[:, 256:384]
    has_tissue = tissue_row > 0.5
    low64 = iota((64, 128), 1) < HD

    acopies = {}
    zcopies = []
    chunks = (3, 2, 1, 0)

    def pass_on(j):
        acopies.pop((0, j)).wait_recv()
        part = att.at[left, chunks[j], 0:96]
        acopies[2, j] = go(part, part, axs.at[2, j], axr.at[2, j], s, right)
        acopies.pop((1, j)).wait_recv()
        part = att.at[right, chunks[j], 96:192]
        acopies[3, j] = go(part, part, axs.at[3, j], axr.at[3, j], s, left)

    def finish(j):
        acopies[2, j].wait_recv()
        acopies[3, j].wait_recv()
        output_rows(chunks[j], att, wrecv, wlast, zout, low64)
        for k in range(4 * chunks[j], 4 * chunks[j] + 4):
            if k:
                to = lax.rem(z - steps[k] + NZ, NZ)
                zcopies.append(
                    go(zout.at[k], zin.at[z], zas.at[k], zar.at[k], to * NQ + q, x)
                )

    for j in range(4):
        chunk = chunks[j]
        at = chunk * 128
        query = qkv[at : at + 128]
        query01 = (query[:, 0:128].astype(F32) * (HD**-0.5)).astype(BF16)
        query2 = (query[:, 384:512].astype(F32) * (HD**-0.5)).astype(BF16)
        row = iota((128, 1), 0) + at
        n_mine = order_of(row, z)
        slide_mine = jnp.zeros((128, 1), jnp.int32)
        end = jnp.int32(0)
        for k in range(8):
            end = end + lens[k]
            slide_mine = slide_mine + jnp.where(n_mine * 128 + c >= end, 1, 0)
        base_ok = (slide_mine == slide_row) & (has_tissue | (row == iota((128, 512), 1)))
        parts = []
        for h in range(3):
            step = (jnp.int32(1) << lax.rem(3 * x + h, 4)) - 1
            allowed = base_ok & ((n_mine & step) == (n_row & step))
            sc = nt(query01 if h < 2 else query2, (key0, key1, key_value2)[h])
            sc = jnp.where(allowed, sc, NEG)
            ex = jnp.exp(sc - jnp.max(sc, axis=1, keepdims=True))
            total = jnp.sum(ex, axis=1, keepdims=True)
            parts.append(mm(ex.astype(BF16), values01 if h < 2 else key_value2) / total)
        att[x, chunk, 0:128] = jnp.where(low128, parts[0], parts[1]).astype(BF16)
        att[x, chunk, 128:192] = jnp.where(
            low64, pltpu.roll(parts[2][0:64], 64, 1), parts[2][64:128]
        ).astype(BF16)
        part = att.at[x, chunk]
        acopies[0, j] = go(part, part, axs.at[0, j], axr.at[0, j], s, right)
        acopies[1, j] = go(part, part, axs.at[1, j], axr.at[1, j], s, left)
        if j >= 2:
            pass_on(j - 2)
    finish(0)
    pass_on(2)
    finish(1)
    pass_on(3)
    finish(2)
    finish(3)
    zin[z] = zout[0]

    for copy in gcopies + rcopies:
        copy.wait_recv()
    gown[:, 0:128] = gown[:, 0:128] + gprev[...].astype(F32)
    gown[:, 384:512] = gown[:, 384:512] + gnext[...].astype(F32)
    out_grad[...] = gown[...].astype(BF16)
    total = rin[0].astype(F32)
    for g in range(1, NX):
        total = total + rin[g].astype(F32)
    out_region[...] = total[:, 0:192].astype(BF16)

    for copy in zcopies:
        copy.wait_recv()
    rows_a = mm(perm_a[...], zin[:, 0:32].reshape(512, 128)).astype(BF16)
    rows_b = mm(perm_b[...], zin[:, 32:48].reshape(256, 128)).astype(BF16)
    pout[:, 0:64] = rows_a.reshape(NQ, 64, 128)
    pout[:, 64:96] = rows_b.reshape(NQ, 32, 128)
    backs = []
    for d in range(1, NQ):
        to = lax.rem(q + d, NQ)
        backs.append(go(pout.at[to], pin.at[q], pbs.at[d], pbr.at[d], z * NQ + to, x))
    pin[q] = pout[q]
    for copy in backs:
        copy.wait_recv()
    for p in range(NQ):
        half = pin[p, 64:96].astype(F32)
        turned = pltpu.roll(half, 64, 1)
        for i in range(4):
            at = i * 128 + p * 16
            k = (i & 1) * 16
            rows_out[at : at + 16, 0:128] = pin[p, 16 * i : 16 * i + 16].astype(F32)
            rows_out[at : at + 16, 128:256] = (half if i < 2 else turned)[k : k + 16]
    for i in range(4):
        at = i * 128
        out_tile[0:128, at : at + 128] = jnp.transpose(rows_out[at : at + 128, 0:128]).astype(BF16)
        out_tile[128:192, at : at + 128] = jnp.transpose(rows_out[at : at + 128, 128:256])[
            0:64
        ].astype(BF16)
    for copy in sent:
        copy.wait_send()


def blocks_of(wide, out):
    for g in range(NX):
        at = g * 192 - (g & 1) * 64
        piece = wide[:, at : at + 256]
        out[g] = (pltpu.roll(piece, 192, 1) if g & 1 else piece).astype(BF16)


def w_out_rows(wcopies, wrecv, wlast):
    for copy in wcopies:
        copy.wait_recv()
    wlast[:, 64:128] = wrecv[:, 128:192]


def output_rows(chunk, att, wrecv, wlast, zout, low64):
    acc = jnp.zeros((128, 256), F32)
    upper = jnp.zeros((64, 256), F32)
    lower = jnp.zeros((64, 256), F32)
    for g in range(NX):
        acc = acc + mm(att[g, chunk, 0:128], wrecv[g, 0:128])
        upper = upper + mm(att[g, chunk, 128:192], wlast[g, 64:192])
        lower = lower + mm(att[g, chunk, 128:192], wlast[g, 0:128])
    acc = acc + jnp.concatenate([upper, lower], axis=0)
    two = acc[:, 128:256].reshape(4, 2, 16, 128)
    packed = jnp.where(
        low64,
        two[:, 0].reshape(64, 128),
        pltpu.roll(two[:, 1].reshape(64, 128), 64, 1),
    )
    at = chunk * 4
    zout[at : at + 4, 0:32] = acc[:, 0:128].reshape(4, 32, 128).astype(BF16)
    zout[at : at + 4, 32:48] = packed.reshape(4, 16, 128).astype(BF16)


def body(
    tile_rows,
    tissue_mask,
    slide_lengths,
    region_rows,
    parent_lists,
    child_counts,
    region_cotangent,
    w_query,
    w_key,
    w_value,
    w_output,
    w_cross_query,
    w_cross_output,
):
    dma = pltpu.SemaphoreType.DMA
    vmem = lambda *shape: pltpu.VMEM(shape, BF16)
    tile_t, region, grad_t = pl.pallas_call(
        kernel,
        out_shape=(
            jax.ShapeDtypeStruct((192, 512), BF16),
            jax.ShapeDtypeStruct((32, 192), BF16),
            jax.ShapeDtypeStruct((192, 512), BF16),
        ),
        in_specs=[pl.BlockSpec(memory_space=pl.ANY)] * 13,
        out_specs=(pl.BlockSpec(memory_space=pltpu.VMEM),) * 3,
        scratch_shapes=[
            vmem(512, 768),
            pltpu.VMEM((512, 128), jnp.int32),
            vmem(32, 768),
            pltpu.VMEM((16, 32), jnp.int32),
            pltpu.VMEM((1, 32), jnp.int32),
            vmem(32, 768),
            pltpu.SMEM((8,), jnp.int32),
            vmem(640, 768),
            vmem(192, 768),
            vmem(256, 768),
            vmem(192, 768),
            vmem(4, 192, 256),
            vmem(128, 768),
            vmem(16, 16, 384),
            vmem(4, 16, 16, 384),
            vmem(512, 640),
            vmem(768, 384),
            vmem(4, 192, 256),
            vmem(4, 192, 256),
            vmem(4, 4, 192, 128),
            vmem(16, 48, 128),
            vmem(16, 48, 128),
            vmem(8, 96, 128),
            vmem(8, 96, 128),
            vmem(2, 192, 128),
            pltpu.VMEM((192, 512), F32),
            vmem(192, 128),
            vmem(192, 128),
            vmem(4, 32, 256),
            vmem(4, 32, 256),
            vmem(512, 512),
            vmem(256, 256),
            pltpu.VMEM((512, 256), F32),
            dma((16,)),
            dma((8,)),
            dma((8,)),
            dma((16,)),
            dma((16,)),
            dma((4, 4)),
            dma((4, 4)),
            dma((4,)),
            dma((4,)),
            dma((2,)),
            dma((2,)),
            dma((4, 4)),
            dma((4, 4)),
            dma((16,)),
            dma((16,)),
            dma((8,)),
            dma((8,)),
            dma((2,)),
            dma((2,)),
            dma((4,)),
            dma((4,)),
        ],
        compiler_params=pltpu.CompilerParams(
            collective_id=0, has_side_effects=True, vmem_limit_bytes=60 * 1024 * 1024
        ),
    )(
        slide_lengths,
        tile_rows,
        tissue_mask.reshape(512, 128),
        region_rows,
        parent_lists.T,
        child_counts.reshape(1, 32),
        region_cotangent,
        w_query.T,
        w_key.T,
        w_value.T,
        w_output,
        w_cross_query.T,
        w_cross_output,
    )
    return tile_t.T, region, grad_t.T


def solution(mesh):
    in_specs = (
        P("seq", None),
        P(),
        P(),
        P("seq", None),
        P("seq", None),
        P("seq"),
        P("seq", None),
        P(None, "head"),
        P(None, "head"),
        P(None, "head"),
        P("head", None),
        P(None, "head"),
        P("head", None),
    )
    out_specs = (P("seq", "head"), P("seq", "head"), P("seq", "head"))
    return jax.shard_map(body, mesh=mesh, in_specs=in_specs, out_specs=out_specs, check_vma=False)
```

```python
import functools

import jax
import jax.numpy as jnp
from jax import lax
from jax.experimental import pallas as pl
from jax.experimental.pallas import tpu as pltpu
from jax.sharding import PartitionSpec as P

HD = 64
NZ = 16
NQ = 8
NX = 4
MESH = pl.DeviceIdType.MESH
F32 = jnp.float32
BF16 = jnp.bfloat16
NEG = -1e30
ZORDER = (1, 15, 2, 14, 3, 13, 4, 12, 5, 11, 6, 10, 7, 9, 8)


def iota(shape, dim):
    return lax.broadcasted_iota(jnp.int32, shape, dim)


def nt(a, b):
    return lax.dot_general(a, b, (((1,), (1,)), ((), ())), preferred_element_type=F32)


def tn(a, b):
    return lax.dot_general(a, b, (((0,), (0,)), ((), ())), preferred_element_type=F32)


def mm(a, b):
    return jnp.dot(a, b, preferred_element_type=F32)


def order_of(row, z):
    k = row >> 5
    near = (k + 1) >> 1
    zk = (z + jnp.where((k & 1) == 1, -near, near)) & (NZ - 1)
    return (zk << 5) | ((row & 7) << 2) | ((row >> 3) & 3)


def kernel(
    lengths,
    tiles,
    tissue,
    regions,
    parents,
    counts,
    cotangent,
    wq_t,
    wk_t,
    wv_t,
    wo,
    wcq_t,
    wco,
    out_tile,
    out_region,
    out_grad,
    tiles_in,
    tissue_in,
    regions_in,
    parents_in,
    counts_in,
    cot_in,
    lens,
    w_t,
    wo_in,
    wcq_in,
    wco_in,
    wout,
    first,
    second,
    feats,
    qkv,
    ext,
    wrecv,
    wlast,
    att,
    zout,
    zin,
    pout,
    pin,
    gext,
    gown,
    gprev,
    gnext,
    rout,
    rin,
    perm_a,
    perm_b,
    rows_out,
    loads,
    p1s,
    p1r,
    p2s,
    p2r,
    pxs,
    pxr,
    wos,
    wor,
    has,
    har,
    axs,
    axr,
    zas,
    zar,
    pbs,
    pbr,
    grs,
    grr,
    res,
    rer,
):
    s = lax.axis_index("seq")
    x = lax.axis_index("head")
    z = s // NQ
    q = lax.rem(s, NQ)
    n_seq = NZ * NQ
    after = lax.rem(s + 1, n_seq)
    before = lax.rem(s + n_seq - 1, n_seq)

    def remote(src, dst, ss, rs, seq, head):
        return pltpu.make_async_remote_copy(
            src_ref=src,
            dst_ref=dst,
            send_sem=ss,
            recv_sem=rs,
            device_id={"seq": seq, "head": head},
            device_id_type=MESH,
        )

    sent = []

    def go(*args):
        copy = remote(*args)
        copy.start()
        sent.append(copy)
        return copy

    barrier = pltpu.get_barrier_semaphore()

    def greet(seq, head):
        pl.semaphore_signal(
            barrier, inc=1, device_id={"seq": seq, "head": head}, device_id_type=MESH
        )

    for d in range(1, NQ):
        greet(z * NQ + lax.rem(q + d, NQ), x)
    for d in ZORDER:
        greet(lax.rem(z + d, NZ) * NQ + q, x)
    for d in range(1, NX):
        greet(s, lax.rem(x + d, NX))
    greet(after, x)
    greet(before, x)
    pl.semaphore_wait(barrier, (NQ - 1) + (NZ - 1) + (NX - 1) + 2)

    hop1 = []
    for d in range(1, NQ):
        to = lax.rem(q + d, NQ)
        hop1.append(
            go(
                tiles.at[pl.ds(pl.multiple_of(x * 128 + to * 16, 16), 16)],
                first.at[pl.ds(pl.multiple_of(q * 16, 16), 16)],
                p1s.at[d],
                p1r.at[d],
                z * NQ + to,
                x,
            )
        )
    local = []

    def load(src, dst):
        copy = pltpu.make_async_copy(src, dst, loads.at[len(local)])
        copy.start()
        local.append(copy)
        return copy

    load_tiles = load(tiles, tiles_in)
    load_w = [
        load(wk_t.at[0:128], w_t.at[128:256]),
        load(wv_t.at[0:128], w_t.at[256:384]),
        load(wk_t.at[128:192], w_t.at[512:576]),
        load(wv_t.at[128:192], w_t.at[576:640]),
        load(wq_t.at[0:128], w_t.at[0:128]),
        load(wq_t.at[128:192], w_t.at[384:448]),
    ]
    load_wo = load(wo, wo_in)
    load_wcq = load(wcq_t, wcq_in.at[0:192])
    load_wco = load(wco, wco_in)
    load_regions = [
        load(regions, regions_in),
        load(parents, parents_in),
        load(counts, counts_in),
        load(cotangent, cot_in),
    ]
    load_mask = [load(tissue, tissue_in), load(lengths, lens)]


    load_wo.wait()
    blocks_of(wo_in[...].astype(F32), wout)
    wcopies = []
    for d in range(1, NX):
        to = lax.rem(x + d, NX)
        wcopies.append(go(wout.at[to], wrecv.at[x], wos.at[d], wor.at[d], s, to))
    wrecv[x] = wout[x]

    load_tiles.wait()
    for copy in load_w:
        copy.wait()
    w_t[448:512] = jnp.zeros((64, 768), BF16)
    first[pl.ds(pl.multiple_of(q * 16, 16), 16), :] = tiles_in[
        pl.ds(pl.multiple_of(x * 128 + q * 16, 16), 16), :
    ]
    block = tiles_in[...]
    ext[128:640, 0:256] = nt(block, w_t[128:384]).astype(BF16)
    ext[128:640, 256:384] = nt(block, w_t[512:640]).astype(BF16)
    halos = [
        go(ext.at[128:256], ext.at[640:768], has.at[0], har.at[0], before, x),
        go(ext.at[512:640], ext.at[0:128], has.at[1], har.at[1], after, x),
    ]

    lane = iota((256, 128), 1)
    row = iota((256, 128), 0)
    source = (lane & 15) * 16 + (lane >> 4)
    turn0 = (source == row).astype(BF16)
    turn1 = (source + 8 == row).astype(BF16)
    for copy in hop1:
        copy.wait_recv()
    second[...] = (
        (mm(turn0, first[:, 0:384]) + mm(turn1, first[:, 384:768]))
        .astype(BF16)
        .reshape(NZ, 16, 384)
    )
    steps = (0,) + ZORDER
    hop2 = {}
    for k in range(1, NZ):
        to = lax.rem(z + steps[k], NZ)
        hop2[k] = go(second.at[to], feats.at[x, k], p2s.at[k], p2r.at[k], to * NQ + q, x)
    feats[x, 0] = second[z]

    peers = [lax.rem(x + e, NX) for e in (1, 3, 2)]
    hopx = {}

    def spread(b):
        for b in (2 * b, 2 * b + 1):
            for k in range(2 * b, 2 * b + 2):
                if k:
                    hop2[k].wait_recv()
            part = feats.at[x, 2 * b : 2 * b + 2]
            for e, to in enumerate(peers):
                hopx[e, b] = go(part, part, pxs.at[e, b], pxr.at[e, b], s, to)

    def project(b):
        for e in range(3):
            hopx[e, 2 * b].wait_recv()
            hopx[e, 2 * b + 1].wait_recv()
        part = [feats[i, k].astype(F32) for k in range(4 * b, 4 * b + 4) for i in range(NX)]
        upper = jnp.concatenate([p[0:8] for p in part], axis=0).astype(BF16)
        lower = jnp.concatenate([p[8:16] for p in part], axis=0).astype(BF16)
        qkv[128 * b : 128 * b + 128] = (
            nt(upper, w_t[:, 0:384]) + nt(lower, w_t[:, 384:768])
        ).astype(BF16)

    low = iota((32, 128), 1) < HD
    load_wcq.wait()
    load_wco.wait()
    for copy in load_regions:
        copy.wait()
    rows32 = regions_in[...]
    wcq_in[192:256] = jnp.zeros((64, 768), BF16)
    cq = nt(rows32, wcq_in[...]).astype(BF16).astype(F32) * (HD**-0.5)
    rk = nt(rows32, w_t[128:384]).astype(BF16).astype(F32)
    rkv2 = nt(rows32, w_t[512:640]).astype(BF16).astype(F32)
    rk01, rv01 = rk[:, 0:128], rk[:, 128:256]
    cq0 = jnp.where(low, cq[:, 0:128], 0.0)
    cq1 = jnp.where(low, 0.0, cq[:, 0:128])
    cq2 = jnp.where(low, cq[:, 128:256], 0.0)
    back_t = nt(wco_in[...], cot_in[...]).astype(BF16)
    place = iota((32, 768), 1)
    times = jnp.zeros((32, 768), F32)
    base = s * 512 - 128
    lists = jnp.where(iota((16, 32), 0) < counts_in[...], parents_in[...] - base, -1)
    lists = jnp.transpose(lists.astype(F32)).astype(jnp.int32)
    for j in range(16):
        times = times + jnp.where(lists[:, j : j + 1] == place, 1.0, 0.0)
    valid = times > 0.0
    for copy in halos:
        copy.wait_recv()
    outs = []
    for h in range(3):
        query = (cq0, cq1, cq2)[h]
        own = jnp.sum(query * (rk01 if h < 2 else rkv2), axis=1, keepdims=True)
        keys = ext[:, 0:128] if h < 2 else ext[:, 256:384]
        values = ext[:, 128:256] if h < 2 else keys
        sc = jnp.where(valid, nt(query.astype(BF16), keys), NEG)
        top = jnp.maximum(own, jnp.max(sc, axis=1, keepdims=True))
        ex = jnp.where(valid, jnp.exp(sc - top), 0.0)
        ex_own = jnp.exp(own - top)
        total = ex_own + jnp.sum(times * ex, axis=1, keepdims=True)
        weight = (ex / total).astype(BF16).astype(F32)
        weight_own = (ex_own / total).astype(BF16).astype(F32)
        mixed = (times * weight).astype(BF16)
        outs.append(mm(mixed, values) + weight_own * (rv01 if h < 2 else rkv2))
        grad = mm(back_t[64 * h : 64 * h + 64], mixed)
        gown[64 * h : 64 * h + 64] = grad[:, 128:640]
        gext[0, 64 * h : 64 * h + 64] = grad[:, 0:128].astype(BF16)
        gext[1, 64 * h : 64 * h + 64] = grad[:, 640:768].astype(BF16)
    cross_a = jnp.where(low, outs[0], outs[1]).astype(BF16)
    cross_b = pltpu.roll(outs[2], 64, 1)[:, 0:64].astype(BF16)
    gcopies = [
        go(gext.at[0], gnext, grs.at[0], grr.at[0], before, x),
        go(gext.at[1], gprev, grs.at[1], grr.at[1], after, x),
    ]
    blocks_of(mm(cross_a, wco_in[0:128]) + mm(cross_b, wco_in[128:192]), rout)
    rcopies = []
    for d in range(1, NX):
        to = lax.rem(x + d, NX)
        rcopies.append(go(rout.at[to], rin.at[x], res.at[d], rer.at[d], s, to))
    rin[x] = rout[x]

    spread(0)

    prow = iota((512, 512), 0)
    pcol = iota((512, 512), 1)
    perm_a[...] = (
        ((prow & 15) * 32 + ((prow >> 4) & 3) * 8 + (prow >> 6)) == pcol
    ).astype(BF16)
    prow = iota((256, 256), 0)
    pcol = iota((256, 256), 1)
    perm_b[...] = (
        ((prow & 15) * 16 + ((prow >> 4) & 1) * 8 + (prow >> 5)) == pcol
    ).astype(BF16)
    wlast[:, 0:64] = jnp.zeros((NX, 64, 256), BF16)
    wlast[:, 128:192] = jnp.zeros((NX, 64, 256), BF16)

    c = q * NZ + z
    for copy in load_mask:
        copy.wait()
    pick = (iota((16, 128), 1) == c).astype(BF16)
    tissue_n = nt(pick, tissue_in[...].astype(F32).astype(BF16)).astype(BF16)
    spread_n = (iota((512, 512), 0) == order_of(iota((512, 512), 1), z)).astype(BF16)
    tissue_row = mm(tissue_n, spread_n)[0:1]
    n_row = order_of(iota((1, 512), 1), z)
    slide_row = jnp.zeros((1, 512), jnp.int32)
    end = jnp.int32(0)
    for k in range(8):
        end = end + lens[k]
        slide_row = slide_row + jnp.where(n_row * 128 + c >= end, 1, 0)

    spread(1)
    w_out_rows(wcopies, wrecv, wlast)
    spread(2)
    project(0)
    spread(3)
    project(1)
    project(2)
    project(3)
    every = qkv[...]

    low128 = iota((128, 128), 1) < HD
    keys01 = every[:, 128:256].astype(F32)
    low512 = iota((512, 128), 1) < HD
    key0 = jnp.where(low512, keys01, 0.0).astype(BF16)
    key1 = jnp.where(low512, 0.0, keys01).astype(BF16)
    key_value2 = every[:, 512:640]
    values01 = every[:, 256:384]
    has_tissue = tissue_row > 0.5
    low64 = iota((64, 128), 1) < HD

    acopies = {}
    zcopies = []
    chunks = (3, 2, 1, 0)

    def finish(j):
        for e in range(3):
            acopies[e, j].wait_recv()
        output_rows(chunks[j], att, wrecv, wlast, zout, low64)
        for k in range(4 * chunks[j], 4 * chunks[j] + 4):
            if k:
                to = lax.rem(z - steps[k] + NZ, NZ)
                zcopies.append(
                    go(zout.at[k], zin.at[z], zas.at[k], zar.at[k], to * NQ + q, x)
                )

    for j in range(4):
        chunk = chunks[j]
        at = chunk * 128
        query = qkv[at : at + 128]
        query01 = (query[:, 0:128].astype(F32) * (HD**-0.5)).astype(BF16)
        query2 = (query[:, 384:512].astype(F32) * (HD**-0.5)).astype(BF16)
        row = iota((128, 1), 0) + at
        n_mine = order_of(row, z)
        slide_mine = jnp.zeros((128, 1), jnp.int32)
        end = jnp.int32(0)
        for k in range(8):
            end = end + lens[k]
            slide_mine = slide_mine + jnp.where(n_mine * 128 + c >= end, 1, 0)
        base_ok = (slide_mine == slide_row) & (has_tissue | (row == iota((128, 512), 1)))
        parts = []
        for h in range(3):
            step = (jnp.int32(1) << lax.rem(3 * x + h, 4)) - 1
            allowed = base_ok & ((n_mine & step) == (n_row & step))
            sc = nt(query01 if h < 2 else query2, (key0, key1, key_value2)[h])
            sc = jnp.where(allowed, sc, NEG)
            ex = jnp.exp(sc - jnp.max(sc, axis=1, keepdims=True))
            total = jnp.sum(ex, axis=1, keepdims=True)
            parts.append(mm(ex.astype(BF16), values01 if h < 2 else key_value2) / total)
        att[x, chunk, 0:128] = jnp.where(low128, parts[0], parts[1]).astype(BF16)
        att[x, chunk, 128:192] = jnp.where(
            low64, pltpu.roll(parts[2][0:64], 64, 1), parts[2][64:128]
        ).astype(BF16)
        part = att.at[x, chunk]
        for e, to in enumerate(peers):
            acopies[e, j] = go(part, part, axs.at[e, j], axr.at[e, j], s, to)
    finish(0)
    finish(1)
    finish(2)
    finish(3)
    zin[z] = zout[0]

    for copy in gcopies + rcopies:
        copy.wait_recv()
    gown[:, 0:128] = gown[:, 0:128] + gprev[...].astype(F32)
    gown[:, 384:512] = gown[:, 384:512] + gnext[...].astype(F32)
    out_grad[...] = gown[...].astype(BF16)
    total = rin[0].astype(F32)
    for g in range(1, NX):
        total = total + rin[g].astype(F32)
    out_region[...] = total[:, 0:192].astype(BF16)

    for copy in zcopies:
        copy.wait_recv()
    rows_a = mm(perm_a[...], zin[:, 0:32].reshape(512, 128)).astype(BF16)
    rows_b = mm(perm_b[...], zin[:, 32:48].reshape(256, 128)).astype(BF16)
    pout[:, 0:64] = rows_a.reshape(NQ, 64, 128)
    pout[:, 64:96] = rows_b.reshape(NQ, 32, 128)
    backs = []
    for d in range(1, NQ):
        to = lax.rem(q + d, NQ)
        backs.append(go(pout.at[to], pin.at[q], pbs.at[d], pbr.at[d], z * NQ + to, x))
    pin[q] = pout[q]
    for copy in backs:
        copy.wait_recv()
    for p in range(NQ):
        half = pin[p, 64:96].astype(F32)
        turned = pltpu.roll(half, 64, 1)
        for i in range(4):
            at = i * 128 + p * 16
            k = (i & 1) * 16
            rows_out[at : at + 16, 0:128] = pin[p, 16 * i : 16 * i + 16].astype(F32)
            rows_out[at : at + 16, 128:256] = (half if i < 2 else turned)[k : k + 16]
    for i in range(4):
        at = i * 128
        out_tile[0:128, at : at + 128] = jnp.transpose(rows_out[at : at + 128, 0:128]).astype(BF16)
        out_tile[128:192, at : at + 128] = jnp.transpose(rows_out[at : at + 128, 128:256])[
            0:64
        ].astype(BF16)
    for copy in sent:
        copy.wait_send()


def blocks_of(wide, out):
    for g in range(NX):
        at = g * 192 - (g & 1) * 64
        piece = wide[:, at : at + 256]
        out[g] = (pltpu.roll(piece, 192, 1) if g & 1 else piece).astype(BF16)


def w_out_rows(wcopies, wrecv, wlast):
    for copy in wcopies:
        copy.wait_recv()
    wlast[:, 64:128] = wrecv[:, 128:192]


def output_rows(chunk, att, wrecv, wlast, zout, low64):
    acc = jnp.zeros((128, 256), F32)
    upper = jnp.zeros((64, 256), F32)
    lower = jnp.zeros((64, 256), F32)
    for g in range(NX):
        acc = acc + mm(att[g, chunk, 0:128], wrecv[g, 0:128])
        upper = upper + mm(att[g, chunk, 128:192], wlast[g, 64:192])
        lower = lower + mm(att[g, chunk, 128:192], wlast[g, 0:128])
    acc = acc + jnp.concatenate([upper, lower], axis=0)
    two = acc[:, 128:256].reshape(4, 2, 16, 128)
    packed = jnp.where(
        low64,
        two[:, 0].reshape(64, 128),
        pltpu.roll(two[:, 1].reshape(64, 128), 64, 1),
    )
    at = chunk * 4
    zout[at : at + 4, 0:32] = acc[:, 0:128].reshape(4, 32, 128).astype(BF16)
    zout[at : at + 4, 32:48] = packed.reshape(4, 16, 128).astype(BF16)


def body(
    tile_rows,
    tissue_mask,
    slide_lengths,
    region_rows,
    parent_lists,
    child_counts,
    region_cotangent,
    w_query,
    w_key,
    w_value,
    w_output,
    w_cross_query,
    w_cross_output,
):
    dma = pltpu.SemaphoreType.DMA
    vmem = lambda *shape: pltpu.VMEM(shape, BF16)
    tile_t, region, grad_t = pl.pallas_call(
        kernel,
        out_shape=(
            jax.ShapeDtypeStruct((192, 512), BF16),
            jax.ShapeDtypeStruct((32, 192), BF16),
            jax.ShapeDtypeStruct((192, 512), BF16),
        ),
        in_specs=[pl.BlockSpec(memory_space=pl.ANY)] * 13,
        out_specs=(pl.BlockSpec(memory_space=pltpu.VMEM),) * 3,
        scratch_shapes=[
            vmem(512, 768),
            pltpu.VMEM((512, 128), jnp.int32),
            vmem(32, 768),
            pltpu.VMEM((16, 32), jnp.int32),
            pltpu.VMEM((1, 32), jnp.int32),
            vmem(32, 768),
            pltpu.SMEM((8,), jnp.int32),
            vmem(640, 768),
            vmem(192, 768),
            vmem(256, 768),
            vmem(192, 768),
            vmem(4, 192, 256),
            vmem(128, 768),
            vmem(16, 16, 384),
            vmem(4, 16, 16, 384),
            vmem(512, 640),
            vmem(768, 384),
            vmem(4, 192, 256),
            vmem(4, 192, 256),
            vmem(4, 4, 192, 128),
            vmem(16, 48, 128),
            vmem(16, 48, 128),
            vmem(8, 96, 128),
            vmem(8, 96, 128),
            vmem(2, 192, 128),
            pltpu.VMEM((192, 512), F32),
            vmem(192, 128),
            vmem(192, 128),
            vmem(4, 32, 256),
            vmem(4, 32, 256),
            vmem(512, 512),
            vmem(256, 256),
            pltpu.VMEM((512, 256), F32),
            dma((16,)),
            dma((8,)),
            dma((8,)),
            dma((16,)),
            dma((16,)),
            dma((4, 8)),
            dma((4, 8)),
            dma((4,)),
            dma((4,)),
            dma((2,)),
            dma((2,)),
            dma((4, 4)),
            dma((4, 4)),
            dma((16,)),
            dma((16,)),
            dma((8,)),
            dma((8,)),
            dma((2,)),
            dma((2,)),
            dma((4,)),
            dma((4,)),
        ],
        compiler_params=pltpu.CompilerParams(
            collective_id=0, has_side_effects=True, vmem_limit_bytes=60 * 1024 * 1024
        ),
    )(
        slide_lengths,
        tile_rows,
        tissue_mask.reshape(512, 128),
        region_rows,
        parent_lists.T,
        child_counts.reshape(1, 32),
        region_cotangent,
        w_query.T,
        w_key.T,
        w_value.T,
        w_output,
        w_cross_query.T,
        w_cross_output,
    )
    return tile_t.T, region, grad_t.T


def solution(mesh):
    in_specs = (
        P("seq", None),
        P(),
        P(),
        P("seq", None),
        P("seq", None),
        P("seq"),
        P("seq", None),
        P(None, "head"),
        P(None, "head"),
        P(None, "head"),
        P("head", None),
        P(None, "head"),
        P("head", None),
    )
    out_specs = (P("seq", "head"), P("seq", "head"), P("seq", "head"))
    return jax.shard_map(body, mesh=mesh, in_specs=in_specs, out_specs=out_specs, check_vma=False)
```

```python
import functools

import jax
import jax.numpy as jnp
from jax import lax
from jax.experimental import pallas as pl
from jax.experimental.pallas import tpu as pltpu
from jax.sharding import PartitionSpec as P

HD = 64
NZ = 16
NQ = 8
NX = 4
MESH = pl.DeviceIdType.MESH
F32 = jnp.float32
BF16 = jnp.bfloat16
NEG = -1e30
ZORDER = (1, 15, 2, 14, 3, 13, 4, 12, 5, 11, 6, 10, 7, 9, 8)


def iota(shape, dim):
    return lax.broadcasted_iota(jnp.int32, shape, dim)


def nt(a, b):
    return lax.dot_general(a, b, (((1,), (1,)), ((), ())), preferred_element_type=F32)


def tn(a, b):
    return lax.dot_general(a, b, (((0,), (0,)), ((), ())), preferred_element_type=F32)


def mm(a, b):
    return jnp.dot(a, b, preferred_element_type=F32)


def order_of(row, z):
    k = row >> 5
    near = (k + 1) >> 1
    zk = (z + jnp.where((k & 1) == 1, -near, near)) & (NZ - 1)
    return (zk << 5) | ((row & 7) << 2) | ((row >> 3) & 3)


def kernel(
    lengths,
    tiles,
    tissue,
    regions,
    parents,
    counts,
    cotangent,
    wq_t,
    wk_t,
    wv_t,
    wo,
    wcq_t,
    wco,
    pin,
    out_region,
    out_grad,
    tiles_in,
    tissue_in,
    regions_in,
    parents_in,
    counts_in,
    cot_in,
    lens,
    w_t,
    wo_in,
    wcq_in,
    wco_in,
    wout,
    first,
    second,
    feats,
    qkv,
    ext,
    wrecv,
    wlast,
    att,
    zout,
    zin,
    pout,
    rfin,
    gfin,
    gext,
    gown,
    gprev,
    gnext,
    rout,
    rin,
    perm_a,
    perm_b,
    osem,
    loads,
    p1s,
    p1r,
    p2s,
    p2r,
    pxs,
    pxr,
    wos,
    wor,
    has,
    har,
    axs,
    axr,
    zas,
    zar,
    pbs,
    pbr,
    grs,
    grr,
    res,
    rer,
):
    s = lax.axis_index("seq")
    x = lax.axis_index("head")
    z = s // NQ
    q = lax.rem(s, NQ)
    n_seq = NZ * NQ
    after = lax.rem(s + 1, n_seq)
    before = lax.rem(s + n_seq - 1, n_seq)

    def remote(src, dst, ss, rs, seq, head):
        return pltpu.make_async_remote_copy(
            src_ref=src,
            dst_ref=dst,
            send_sem=ss,
            recv_sem=rs,
            device_id={"seq": seq, "head": head},
            device_id_type=MESH,
        )

    sent = []

    def go(*args):
        copy = remote(*args)
        copy.start()
        sent.append(copy)
        return copy

    barrier = pltpu.get_barrier_semaphore()

    def greet(seq, head):
        pl.semaphore_signal(
            barrier, inc=1, device_id={"seq": seq, "head": head}, device_id_type=MESH
        )

    for d in range(1, NQ):
        greet(z * NQ + lax.rem(q + d, NQ), x)
    for d in ZORDER:
        greet(lax.rem(z + d, NZ) * NQ + q, x)
    for d in range(1, NX):
        greet(s, lax.rem(x + d, NX))
    greet(after, x)
    greet(before, x)
    pl.semaphore_wait(barrier, (NQ - 1) + (NZ - 1) + (NX - 1) + 2)

    hop1 = []
    for d in range(1, NQ):
        to = lax.rem(q + d, NQ)
        hop1.append(
            go(
                tiles.at[pl.ds(pl.multiple_of(x * 128 + to * 16, 16), 16)],
                first.at[pl.ds(pl.multiple_of(q * 16, 16), 16)],
                p1s.at[d],
                p1r.at[d],
                z * NQ + to,
                x,
            )
        )
    local = []

    def load(src, dst):
        copy = pltpu.make_async_copy(src, dst, loads.at[len(local)])
        copy.start()
        local.append(copy)
        return copy

    load_tiles = load(tiles, tiles_in)
    load_w = [
        load(wk_t.at[0:128], w_t.at[128:256]),
        load(wv_t.at[0:128], w_t.at[256:384]),
        load(wk_t.at[128:192], w_t.at[512:576]),
        load(wv_t.at[128:192], w_t.at[576:640]),
        load(wq_t.at[0:128], w_t.at[0:128]),
        load(wq_t.at[128:192], w_t.at[384:448]),
    ]
    load_wo = load(wo, wo_in)
    load_wcq = load(wcq_t, wcq_in.at[0:192])
    load_wco = load(wco, wco_in)
    load_regions = [
        load(regions, regions_in),
        load(parents, parents_in),
        load(counts, counts_in),
        load(cotangent, cot_in),
    ]
    load_mask = [load(tissue, tissue_in), load(lengths, lens)]


    load_wo.wait()
    blocks_of(wo_in[...].astype(F32), wout)
    wcopies = []
    for d in range(1, NX):
        to = lax.rem(x + d, NX)
        wcopies.append(go(wout.at[to], wrecv.at[x], wos.at[d], wor.at[d], s, to))
    wrecv[x] = wout[x]

    load_tiles.wait()
    for copy in load_w:
        copy.wait()
    w_t[448:512] = jnp.zeros((64, 768), BF16)
    first[pl.ds(pl.multiple_of(q * 16, 16), 16), :] = tiles_in[
        pl.ds(pl.multiple_of(x * 128 + q * 16, 16), 16), :
    ]
    block = tiles_in[...]
    ext[128:640, 0:256] = nt(block, w_t[128:384]).astype(BF16)
    ext[128:640, 256:384] = nt(block, w_t[512:640]).astype(BF16)
    halos = [
        go(ext.at[128:256], ext.at[640:768], has.at[0], har.at[0], before, x),
        go(ext.at[512:640], ext.at[0:128], has.at[1], har.at[1], after, x),
    ]

    lane = iota((256, 128), 1)
    row = iota((256, 128), 0)
    source = (lane & 15) * 16 + (lane >> 4)
    turn0 = (source == row).astype(BF16)
    turn1 = (source + 8 == row).astype(BF16)
    for copy in hop1:
        copy.wait_recv()
    second[...] = (
        (mm(turn0, first[:, 0:384]) + mm(turn1, first[:, 384:768]))
        .astype(BF16)
        .reshape(NZ, 16, 384)
    )
    steps = (0,) + ZORDER
    hop2 = {}
    for k in range(1, NZ):
        to = lax.rem(z + steps[k], NZ)
        hop2[k] = go(second.at[to], feats.at[x, k], p2s.at[k], p2r.at[k], to * NQ + q, x)
    feats[x, 0] = second[z]

    peers = [lax.rem(x + e, NX) for e in (1, 3, 2)]
    hopx = {}

    def spread(b):
        for b in (2 * b, 2 * b + 1):
            for k in range(2 * b, 2 * b + 2):
                if k:
                    hop2[k].wait_recv()
            part = feats.at[x, 2 * b : 2 * b + 2]
            for e, to in enumerate(peers):
                hopx[e, b] = go(part, part, pxs.at[e, b], pxr.at[e, b], s, to)

    def project(b):
        for e in range(3):
            hopx[e, 2 * b].wait_recv()
            hopx[e, 2 * b + 1].wait_recv()
        part = [feats[i, k].astype(F32) for k in range(4 * b, 4 * b + 4) for i in range(NX)]
        upper = jnp.concatenate([p[0:8] for p in part], axis=0).astype(BF16)
        lower = jnp.concatenate([p[8:16] for p in part], axis=0).astype(BF16)
        qkv[128 * b : 128 * b + 128] = (
            nt(upper, w_t[:, 0:384]) + nt(lower, w_t[:, 384:768])
        ).astype(BF16)

    low = iota((32, 128), 1) < HD
    load_wcq.wait()
    load_wco.wait()
    for copy in load_regions:
        copy.wait()
    rows32 = regions_in[...]
    wcq_in[192:256] = jnp.zeros((64, 768), BF16)
    cq = nt(rows32, wcq_in[...]).astype(BF16).astype(F32) * (HD**-0.5)
    rk = nt(rows32, w_t[128:384]).astype(BF16).astype(F32)
    rkv2 = nt(rows32, w_t[512:640]).astype(BF16).astype(F32)
    rk01, rv01 = rk[:, 0:128], rk[:, 128:256]
    cq0 = jnp.where(low, cq[:, 0:128], 0.0)
    cq1 = jnp.where(low, 0.0, cq[:, 0:128])
    cq2 = jnp.where(low, cq[:, 128:256], 0.0)
    back_t = nt(wco_in[...], cot_in[...]).astype(BF16)
    place = iota((32, 768), 1)
    times = jnp.zeros((32, 768), F32)
    base = s * 512 - 128
    lists = jnp.where(iota((16, 32), 0) < counts_in[...], parents_in[...] - base, -1)
    lists = jnp.transpose(lists.astype(F32)).astype(jnp.int32)
    for j in range(16):
        times = times + jnp.where(lists[:, j : j + 1] == place, 1.0, 0.0)
    valid = times > 0.0
    for copy in halos:
        copy.wait_recv()
    outs = []
    for h in range(3):
        query = (cq0, cq1, cq2)[h]
        own = jnp.sum(query * (rk01 if h < 2 else rkv2), axis=1, keepdims=True)
        keys = ext[:, 0:128] if h < 2 else ext[:, 256:384]
        values = ext[:, 128:256] if h < 2 else keys
        sc = jnp.where(valid, nt(query.astype(BF16), keys), NEG)
        top = jnp.maximum(own, jnp.max(sc, axis=1, keepdims=True))
        ex = jnp.where(valid, jnp.exp(sc - top), 0.0)
        ex_own = jnp.exp(own - top)
        total = ex_own + jnp.sum(times * ex, axis=1, keepdims=True)
        weight = (ex / total).astype(BF16).astype(F32)
        weight_own = (ex_own / total).astype(BF16).astype(F32)
        mixed = (times * weight).astype(BF16)
        outs.append(mm(mixed, values) + weight_own * (rv01 if h < 2 else rkv2))
        grad = mm(back_t[64 * h : 64 * h + 64], mixed)
        gown[64 * h : 64 * h + 64] = grad[:, 128:640]
        gext[0, 64 * h : 64 * h + 64] = grad[:, 0:128].astype(BF16)
        gext[1, 64 * h : 64 * h + 64] = grad[:, 640:768].astype(BF16)
    cross_a = jnp.where(low, outs[0], outs[1]).astype(BF16)
    cross_b = pltpu.roll(outs[2], 64, 1)[:, 0:64].astype(BF16)
    gcopies = [
        go(gext.at[0], gnext, grs.at[0], grr.at[0], before, x),
        go(gext.at[1], gprev, grs.at[1], grr.at[1], after, x),
    ]
    blocks_of(mm(cross_a, wco_in[0:128]) + mm(cross_b, wco_in[128:192]), rout)
    rcopies = []
    for d in range(1, NX):
        to = lax.rem(x + d, NX)
        rcopies.append(go(rout.at[to], rin.at[x], res.at[d], rer.at[d], s, to))
    rin[x] = rout[x]

    spread(0)

    prow = iota((512, 512), 0)
    pcol = iota((512, 512), 1)
    perm_a[...] = (
        ((prow & 15) * 32 + ((prow >> 4) & 3) * 8 + (prow >> 6)) == pcol
    ).astype(BF16)
    prow = iota((256, 256), 0)
    pcol = iota((256, 256), 1)
    perm_b[...] = (
        ((prow & 15) * 16 + ((prow >> 4) & 1) * 8 + (prow >> 5)) == pcol
    ).astype(BF16)
    wlast[:, 0:64] = jnp.zeros((NX, 64, 256), BF16)
    wlast[:, 128:192] = jnp.zeros((NX, 64, 256), BF16)

    c = q * NZ + z
    for copy in load_mask:
        copy.wait()
    pick = (iota((16, 128), 1) == c).astype(BF16)
    tissue_n = nt(pick, tissue_in[...].astype(F32).astype(BF16)).astype(BF16)
    spread_n = (iota((512, 512), 0) == order_of(iota((512, 512), 1), z)).astype(BF16)
    tissue_row = mm(tissue_n, spread_n)[0:1]
    n_row = order_of(iota((1, 512), 1), z)
    slide_row = jnp.zeros((1, 512), jnp.int32)
    end = jnp.int32(0)
    for k in range(8):
        end = end + lens[k]
        slide_row = slide_row + jnp.where(n_row * 128 + c >= end, 1, 0)

    spread(1)
    w_out_rows(wcopies, wrecv, wlast)
    spread(2)
    project(0)
    spread(3)
    project(1)
    project(2)
    project(3)
    every = qkv[...]

    low128 = iota((128, 128), 1) < HD
    keys01 = every[:, 128:256].astype(F32)
    low512 = iota((512, 128), 1) < HD
    key0 = jnp.where(low512, keys01, 0.0).astype(BF16)
    key1 = jnp.where(low512, 0.0, keys01).astype(BF16)
    key_value2 = every[:, 512:640]
    values01 = every[:, 256:384]
    has_tissue = tissue_row > 0.5
    low64 = iota((64, 128), 1) < HD

    acopies = {}
    zcopies = []
    chunks = (3, 2, 1, 0)

    def finish(j):
        for e in range(3):
            acopies[e, j].wait_recv()
        output_rows(chunks[j], att, wrecv, wlast, zout, low64)
        for k in range(4 * chunks[j], 4 * chunks[j] + 4):
            if k:
                to = lax.rem(z - steps[k] + NZ, NZ)
                zcopies.append(
                    go(zout.at[k], zin.at[z], zas.at[k], zar.at[k], to * NQ + q, x)
                )

    for j in range(4):
        chunk = chunks[j]
        at = chunk * 128
        query = qkv[at : at + 128]
        query01 = (query[:, 0:128].astype(F32) * (HD**-0.5)).astype(BF16)
        query2 = (query[:, 384:512].astype(F32) * (HD**-0.5)).astype(BF16)
        row = iota((128, 1), 0) + at
        n_mine = order_of(row, z)
        slide_mine = jnp.zeros((128, 1), jnp.int32)
        end = jnp.int32(0)
        for k in range(8):
            end = end + lens[k]
            slide_mine = slide_mine + jnp.where(n_mine * 128 + c >= end, 1, 0)
        base_ok = (slide_mine == slide_row) & (has_tissue | (row == iota((128, 512), 1)))
        parts = []
        for h in range(3):
            step = (jnp.int32(1) << lax.rem(3 * x + h, 4)) - 1
            allowed = base_ok & ((n_mine & step) == (n_row & step))
            sc = nt(query01 if h < 2 else query2, (key0, key1, key_value2)[h])
            sc = jnp.where(allowed, sc, NEG)
            ex = jnp.exp(sc - jnp.max(sc, axis=1, keepdims=True))
            total = jnp.sum(ex, axis=1, keepdims=True)
            parts.append(mm(ex.astype(BF16), values01 if h < 2 else key_value2) / total)
        att[x, chunk, 0:128] = jnp.where(low128, parts[0], parts[1]).astype(BF16)
        att[x, chunk, 128:192] = jnp.where(
            low64, pltpu.roll(parts[2][0:64], 64, 1), parts[2][64:128]
        ).astype(BF16)
        part = att.at[x, chunk]
        for e, to in enumerate(peers):
            acopies[e, j] = go(part, part, axs.at[e, j], axr.at[e, j], s, to)
    finish(0)
    finish(1)
    finish(2)
    finish(3)
    zin[z] = zout[0]

    for copy in gcopies + rcopies:
        copy.wait_recv()
    gown[:, 0:128] = gown[:, 0:128] + gprev[...].astype(F32)
    gown[:, 384:512] = gown[:, 384:512] + gnext[...].astype(F32)
    gfin[...] = gown[...].astype(BF16)
    total = rin[0].astype(F32)
    for g in range(1, NX):
        total = total + rin[g].astype(F32)
    rfin[...] = total[:, 0:192].astype(BF16)
    outward = [
        pltpu.make_async_copy(rfin, out_region, osem.at[1]),
        pltpu.make_async_copy(gfin, out_grad, osem.at[2]),
    ]
    for copy in outward:
        copy.start()

    for copy in zcopies:
        copy.wait_recv()
    rows_a = mm(perm_a[...], zin[:, 0:32].reshape(512, 128)).astype(BF16)
    rows_b = mm(perm_b[...], zin[:, 32:48].reshape(256, 128)).astype(BF16)
    pout[:, 0:64] = rows_a.reshape(NQ, 64, 128)
    pout[:, 64:96] = rows_b.reshape(NQ, 32, 128)
    backs = []
    for d in range(1, NQ):
        to = lax.rem(q + d, NQ)
        backs.append(go(pout.at[to], pin.at[q], pbs.at[d], pbr.at[d], z * NQ + to, x))
    own_back = pltpu.make_async_copy(pout.at[q], pin.at[q], osem.at[0])
    own_back.start()
    for copy in backs:
        copy.wait_recv()
    own_back.wait()
    for copy in outward:
        copy.wait()
    for copy in sent:
        copy.wait_send()


def blocks_of(wide, out):
    for g in range(NX):
        at = g * 192 - (g & 1) * 64
        piece = wide[:, at : at + 256]
        out[g] = (pltpu.roll(piece, 192, 1) if g & 1 else piece).astype(BF16)


def w_out_rows(wcopies, wrecv, wlast):
    for copy in wcopies:
        copy.wait_recv()
    wlast[:, 64:128] = wrecv[:, 128:192]


def output_rows(chunk, att, wrecv, wlast, zout, low64):
    acc = jnp.zeros((128, 256), F32)
    upper = jnp.zeros((64, 256), F32)
    lower = jnp.zeros((64, 256), F32)
    for g in range(NX):
        acc = acc + mm(att[g, chunk, 0:128], wrecv[g, 0:128])
        upper = upper + mm(att[g, chunk, 128:192], wlast[g, 64:192])
        lower = lower + mm(att[g, chunk, 128:192], wlast[g, 0:128])
    acc = acc + jnp.concatenate([upper, lower], axis=0)
    two = acc[:, 128:256].reshape(4, 2, 16, 128)
    packed = jnp.where(
        low64,
        two[:, 0].reshape(64, 128),
        pltpu.roll(two[:, 1].reshape(64, 128), 64, 1),
    )
    at = chunk * 4
    zout[at : at + 4, 0:32] = acc[:, 0:128].reshape(4, 32, 128).astype(BF16)
    zout[at : at + 4, 32:48] = packed.reshape(4, 16, 128).astype(BF16)


def assemble(pin, region, grad, out_tile, out_region, out_grad, rows_out):
    out_region[...] = region[...]
    out_grad[...] = grad[...]
    for p in range(NQ):
        half = pin[p, 64:96].astype(F32)
        turned = pltpu.roll(half, 64, 1)
        for i in range(4):
            at = i * 128 + p * 16
            k = (i & 1) * 16
            rows_out[at : at + 16, 0:128] = pin[p, 16 * i : 16 * i + 16].astype(F32)
            rows_out[at : at + 16, 128:256] = (half if i < 2 else turned)[k : k + 16]
    for i in range(4):
        at = i * 128
        out_tile[0:128, at : at + 128] = jnp.transpose(rows_out[at : at + 128, 0:128]).astype(BF16)
        out_tile[128:192, at : at + 128] = jnp.transpose(rows_out[at : at + 128, 128:256])[
            0:64
        ].astype(BF16)


def body(
    tile_rows,
    tissue_mask,
    slide_lengths,
    region_rows,
    parent_lists,
    child_counts,
    region_cotangent,
    w_query,
    w_key,
    w_value,
    w_output,
    w_cross_query,
    w_cross_output,
):
    dma = pltpu.SemaphoreType.DMA
    vmem = lambda *shape: pltpu.VMEM(shape, BF16)
    parts, region, grad_t = pl.pallas_call(
        kernel,
        out_shape=(
            jax.ShapeDtypeStruct((8, 96, 128), BF16),
            jax.ShapeDtypeStruct((32, 192), BF16),
            jax.ShapeDtypeStruct((192, 512), BF16),
        ),
        in_specs=[pl.BlockSpec(memory_space=pl.ANY)] * 13,
        out_specs=(pl.BlockSpec(memory_space=pl.ANY),) * 3,
        scratch_shapes=[
            vmem(512, 768),
            pltpu.VMEM((512, 128), jnp.int32),
            vmem(32, 768),
            pltpu.VMEM((16, 32), jnp.int32),
            pltpu.VMEM((1, 32), jnp.int32),
            vmem(32, 768),
            pltpu.SMEM((8,), jnp.int32),
            vmem(640, 768),
            vmem(192, 768),
            vmem(256, 768),
            vmem(192, 768),
            vmem(4, 192, 256),
            vmem(128, 768),
            vmem(16, 16, 384),
            vmem(4, 16, 16, 384),
            vmem(512, 640),
            vmem(768, 384),
            vmem(4, 192, 256),
            vmem(4, 192, 256),
            vmem(4, 4, 192, 128),
            vmem(16, 48, 128),
            vmem(16, 48, 128),
            vmem(8, 96, 128),
            vmem(32, 192),
            vmem(192, 512),
            vmem(2, 192, 128),
            pltpu.VMEM((192, 512), F32),
            vmem(192, 128),
            vmem(192, 128),
            vmem(4, 32, 256),
            vmem(4, 32, 256),
            vmem(512, 512),
            vmem(256, 256),
            dma((3,)),
            dma((16,)),
            dma((8,)),
            dma((8,)),
            dma((16,)),
            dma((16,)),
            dma((4, 8)),
            dma((4, 8)),
            dma((4,)),
            dma((4,)),
            dma((2,)),
            dma((2,)),
            dma((4, 4)),
            dma((4, 4)),
            dma((16,)),
            dma((16,)),
            dma((8,)),
            dma((8,)),
            dma((2,)),
            dma((2,)),
            dma((4,)),
            dma((4,)),
        ],
        compiler_params=pltpu.CompilerParams(
            collective_id=0, has_side_effects=True, vmem_limit_bytes=60 * 1024 * 1024
        ),
    )(
        slide_lengths,
        tile_rows,
        tissue_mask.reshape(512, 128),
        region_rows,
        parent_lists.T,
        child_counts.reshape(1, 32),
        region_cotangent,
        w_query.T,
        w_key.T,
        w_value.T,
        w_output,
        w_cross_query.T,
        w_cross_output,
    )
    tile_t, region, grad_t = pl.pallas_call(
        assemble,
        out_shape=(
            jax.ShapeDtypeStruct((192, 512), BF16),
            jax.ShapeDtypeStruct((32, 192), BF16),
            jax.ShapeDtypeStruct((192, 512), BF16),
        ),
        scratch_shapes=[pltpu.VMEM((512, 256), F32)],
    )(parts, region, grad_t)
    return tile_t.T, region, grad_t.T


def solution(mesh):
    in_specs = (
        P("seq", None),
        P(),
        P(),
        P("seq", None),
        P("seq", None),
        P("seq"),
        P("seq", None),
        P(None, "head"),
        P(None, "head"),
        P(None, "head"),
        P("head", None),
        P(None, "head"),
        P("head", None),
    )
    out_specs = (P("seq", "head"), P("seq", "head"), P("seq", "head"))
    return jax.shard_map(body, mesh=mesh, in_specs=in_specs, out_specs=out_specs, check_vma=False)
```

```python
import functools

import jax
import jax.numpy as jnp
from jax import lax
from jax.experimental import pallas as pl
from jax.experimental.pallas import tpu as pltpu
from jax.sharding import PartitionSpec as P

HD = 64
NZ = 16
NQ = 8
NX = 4
MESH = pl.DeviceIdType.MESH
F32 = jnp.float32
BF16 = jnp.bfloat16
NEG = -1e30
ZORDER = (1, 15, 2, 14, 3, 13, 4, 12, 5, 11, 6, 10, 7, 9, 8)


def iota(shape, dim):
    return lax.broadcasted_iota(jnp.int32, shape, dim)


def nt(a, b):
    return lax.dot_general(a, b, (((1,), (1,)), ((), ())), preferred_element_type=F32)


def tn(a, b):
    return lax.dot_general(a, b, (((0,), (0,)), ((), ())), preferred_element_type=F32)


def mm(a, b):
    return jnp.dot(a, b, preferred_element_type=F32)


def order_of(row, z):
    k = row >> 5
    near = (k + 1) >> 1
    zk = (z + jnp.where((k & 1) == 1, -near, near)) & (NZ - 1)
    return (zk << 5) | ((row & 7) << 2) | ((row >> 3) & 3)


def kernel(
    lengths,
    tiles,
    tissue,
    regions,
    parents,
    counts,
    cotangent,
    wq_t,
    wk_t,
    wv_t,
    wo,
    wcq_t,
    wco,
    pin,
    out_region,
    out_grad,
    tiles_in,
    tissue_in,
    regions_in,
    parents_in,
    counts_in,
    cot_in,
    lens,
    w_t,
    wo_in,
    wcq_in,
    wco_in,
    wout,
    first,
    second,
    feats,
    qkv,
    ext,
    wrecv,
    wlast,
    att,
    zout,
    zin,
    pout,
    rfin,
    gfin,
    gext,
    gown,
    gprev,
    gnext,
    rout,
    rin,
    perm_a,
    perm_b,
    osem,
    loads,
    p1s,
    p1r,
    p2s,
    p2r,
    pxs,
    pxr,
    wos,
    wor,
    has,
    har,
    axs,
    axr,
    zas,
    zar,
    pbs,
    pbr,
    grs,
    grr,
    res,
    rer,
):
    s = lax.axis_index("seq")
    x = lax.axis_index("head")
    z = s // NQ
    q = lax.rem(s, NQ)
    n_seq = NZ * NQ
    after = lax.rem(s + 1, n_seq)
    before = lax.rem(s + n_seq - 1, n_seq)

    def remote(src, dst, ss, rs, seq, head):
        return pltpu.make_async_remote_copy(
            src_ref=src,
            dst_ref=dst,
            send_sem=ss,
            recv_sem=rs,
            device_id={"seq": seq, "head": head},
            device_id_type=MESH,
        )

    sent = []

    def go(*args):
        copy = remote(*args)
        copy.start()
        sent.append(copy)
        return copy

    barrier = pltpu.get_barrier_semaphore()

    def greet(seq, head):
        pl.semaphore_signal(
            barrier, inc=1, device_id={"seq": seq, "head": head}, device_id_type=MESH
        )

    for d in reversed(ZORDER):
        greet(lax.rem(z + d, NZ) * NQ + q, x)
    greet(after, x)
    greet(before, x)
    for d in range(1, NQ):
        greet(z * NQ + lax.rem(q + d, NQ), x)
    for d in range(1, NX):
        greet(s, lax.rem(x + d, NX))
    pl.semaphore_wait(barrier, (NQ - 1) + (NZ - 1) + (NX - 1) + 2)

    hop1 = []
    for d in range(1, NQ):
        to = lax.rem(q + d, NQ)
        hop1.append(
            go(
                tiles.at[pl.ds(pl.multiple_of(x * 128 + to * 16, 16), 16)],
                first.at[pl.ds(pl.multiple_of(q * 16, 16), 16)],
                p1s.at[d],
                p1r.at[d],
                z * NQ + to,
                x,
            )
        )
    local = []

    def load(src, dst):
        copy = pltpu.make_async_copy(src, dst, loads.at[len(local)])
        copy.start()
        local.append(copy)
        return copy

    load_tiles = load(tiles, tiles_in)
    load_w = [
        load(wk_t.at[0:128], w_t.at[128:256]),
        load(wv_t.at[0:128], w_t.at[256:384]),
        load(wk_t.at[128:192], w_t.at[512:576]),
        load(wv_t.at[128:192], w_t.at[576:640]),
        load(wq_t.at[0:128], w_t.at[0:128]),
        load(wq_t.at[128:192], w_t.at[384:448]),
    ]
    load_wo = load(wo, wo_in)
    load_wcq = load(wcq_t, wcq_in.at[0:192])
    load_wco = load(wco, wco_in)
    load_regions = [
        load(regions, regions_in),
        load(parents, parents_in),
        load(counts, counts_in),
        load(cotangent, cot_in),
    ]
    load_mask = [load(tissue, tissue_in), load(lengths, lens)]


    load_wo.wait()
    blocks_of(wo_in[...].astype(F32), wout)
    wcopies = []
    for d in range(1, NX):
        to = lax.rem(x + d, NX)
        wcopies.append(go(wout.at[to], wrecv.at[x], wos.at[d], wor.at[d], s, to))
    wrecv[x] = wout[x]

    load_tiles.wait()
    for copy in load_w:
        copy.wait()
    w_t[448:512] = jnp.zeros((64, 768), BF16)
    first[pl.ds(pl.multiple_of(q * 16, 16), 16), :] = tiles_in[
        pl.ds(pl.multiple_of(x * 128 + q * 16, 16), 16), :
    ]
    block = tiles_in[...]
    ext[128:640, 0:256] = nt(block, w_t[128:384]).astype(BF16)
    ext[128:640, 256:384] = nt(block, w_t[512:640]).astype(BF16)
    halos = [
        go(ext.at[128:256], ext.at[640:768], has.at[0], har.at[0], before, x),
        go(ext.at[512:640], ext.at[0:128], has.at[1], har.at[1], after, x),
    ]

    lane = iota((256, 128), 1)
    row = iota((256, 128), 0)
    source = (lane & 15) * 16 + (lane >> 4)
    turn0 = (source == row).astype(BF16)
    turn1 = (source + 8 == row).astype(BF16)
    for copy in hop1:
        copy.wait_recv()
    second[...] = (
        (mm(turn0, first[:, 0:384]) + mm(turn1, first[:, 384:768]))
        .astype(BF16)
        .reshape(NZ, 16, 384)
    )
    steps = (0,) + ZORDER
    hop2 = {}
    for k in range(1, NZ):
        to = lax.rem(z + steps[k], NZ)
        hop2[k] = go(second.at[to], feats.at[x, k], p2s.at[k], p2r.at[k], to * NQ + q, x)
    feats[x, 0] = second[z]

    peers = [lax.rem(x + e, NX) for e in (1, 3, 2)]
    hopx = {}

    def spread(b):
        for b in (2 * b, 2 * b + 1):
            for k in range(2 * b, 2 * b + 2):
                if k:
                    hop2[k].wait_recv()
            part = feats.at[x, 2 * b : 2 * b + 2]
            for e, to in enumerate(peers):
                hopx[e, b] = go(part, part, pxs.at[e, b], pxr.at[e, b], s, to)

    def project(b):
        for e in range(3):
            hopx[e, 2 * b].wait_recv()
            hopx[e, 2 * b + 1].wait_recv()
        part = [feats[i, k].astype(F32) for k in range(4 * b, 4 * b + 4) for i in range(NX)]
        upper = jnp.concatenate([p[0:8] for p in part], axis=0).astype(BF16)
        lower = jnp.concatenate([p[8:16] for p in part], axis=0).astype(BF16)
        qkv[128 * b : 128 * b + 128] = (
            nt(upper, w_t[:, 0:384]) + nt(lower, w_t[:, 384:768])
        ).astype(BF16)

    low = iota((32, 128), 1) < HD
    load_wcq.wait()
    load_wco.wait()
    for copy in load_regions:
        copy.wait()
    rows32 = regions_in[...]
    wcq_in[192:256] = jnp.zeros((64, 768), BF16)
    cq = nt(rows32, wcq_in[...]).astype(BF16).astype(F32) * (HD**-0.5)
    rk = nt(rows32, w_t[128:384]).astype(BF16).astype(F32)
    rkv2 = nt(rows32, w_t[512:640]).astype(BF16).astype(F32)
    rk01, rv01 = rk[:, 0:128], rk[:, 128:256]
    cq0 = jnp.where(low, cq[:, 0:128], 0.0)
    cq1 = jnp.where(low, 0.0, cq[:, 0:128])
    cq2 = jnp.where(low, cq[:, 128:256], 0.0)
    back_t = nt(wco_in[...], cot_in[...]).astype(BF16)
    place = iota((32, 768), 1)
    times = jnp.zeros((32, 768), F32)
    base = s * 512 - 128
    lists = jnp.where(iota((16, 32), 0) < counts_in[...], parents_in[...] - base, -1)
    lists = jnp.transpose(lists.astype(F32)).astype(jnp.int32)
    for j in range(16):
        times = times + jnp.where(lists[:, j : j + 1] == place, 1.0, 0.0)
    valid = times > 0.0
    for copy in halos:
        copy.wait_recv()
    outs = []
    for h in range(3):
        query = (cq0, cq1, cq2)[h]
        own = jnp.sum(query * (rk01 if h < 2 else rkv2), axis=1, keepdims=True)
        keys = ext[:, 0:128] if h < 2 else ext[:, 256:384]
        values = ext[:, 128:256] if h < 2 else keys
        sc = jnp.where(valid, nt(query.astype(BF16), keys), NEG)
        top = jnp.maximum(own, jnp.max(sc, axis=1, keepdims=True))
        ex = jnp.where(valid, jnp.exp(sc - top), 0.0)
        ex_own = jnp.exp(own - top)
        total = ex_own + jnp.sum(times * ex, axis=1, keepdims=True)
        weight = (ex / total).astype(BF16).astype(F32)
        weight_own = (ex_own / total).astype(BF16).astype(F32)
        mixed = (times * weight).astype(BF16)
        outs.append(mm(mixed, values) + weight_own * (rv01 if h < 2 else rkv2))
        grad = mm(back_t[64 * h : 64 * h + 64], mixed)
        gown[64 * h : 64 * h + 64] = grad[:, 128:640]
        gext[0, 64 * h : 64 * h + 64] = grad[:, 0:128].astype(BF16)
        gext[1, 64 * h : 64 * h + 64] = grad[:, 640:768].astype(BF16)
    cross_a = jnp.where(low, outs[0], outs[1]).astype(BF16)
    cross_b = pltpu.roll(outs[2], 64, 1)[:, 0:64].astype(BF16)
    gcopies = [
        go(gext.at[0], gnext, grs.at[0], grr.at[0], before, x),
        go(gext.at[1], gprev, grs.at[1], grr.at[1], after, x),
    ]
    blocks_of(mm(cross_a, wco_in[0:128]) + mm(cross_b, wco_in[128:192]), rout)
    rcopies = []
    for d in range(1, NX):
        to = lax.rem(x + d, NX)
        rcopies.append(go(rout.at[to], rin.at[x], res.at[d], rer.at[d], s, to))
    rin[x] = rout[x]

    spread(0)

    prow = iota((512, 512), 0)
    pcol = iota((512, 512), 1)
    perm_a[...] = (
        ((prow & 15) * 32 + ((prow >> 4) & 3) * 8 + (prow >> 6)) == pcol
    ).astype(BF16)
    prow = iota((256, 256), 0)
    pcol = iota((256, 256), 1)
    perm_b[...] = (
        ((prow & 15) * 16 + ((prow >> 4) & 1) * 8 + (prow >> 5)) == pcol
    ).astype(BF16)
    wlast[:, 0:64] = jnp.zeros((NX, 64, 256), BF16)
    wlast[:, 128:192] = jnp.zeros((NX, 64, 256), BF16)

    c = q * NZ + z
    for copy in load_mask:
        copy.wait()
    pick = (iota((16, 128), 1) == c).astype(BF16)
    tissue_n = nt(pick, tissue_in[...].astype(F32).astype(BF16)).astype(BF16)
    spread_n = (iota((512, 512), 0) == order_of(iota((512, 512), 1), z)).astype(BF16)
    tissue_row = mm(tissue_n, spread_n)[0:1]
    n_row = order_of(iota((1, 512), 1), z)
    slide_row = jnp.zeros((1, 512), jnp.int32)
    end = jnp.int32(0)
    for k in range(8):
        end = end + lens[k]
        slide_row = slide_row + jnp.where(n_row * 128 + c >= end, 1, 0)

    spread(1)
    w_out_rows(wcopies, wrecv, wlast)
    spread(2)
    project(0)
    spread(3)
    project(1)
    project(2)
    project(3)
    every = qkv[...]

    low128 = iota((128, 128), 1) < HD
    keys01 = every[:, 128:256].astype(F32)
    low512 = iota((512, 128), 1) < HD
    key0 = jnp.where(low512, keys01, 0.0).astype(BF16)
    key1 = jnp.where(low512, 0.0, keys01).astype(BF16)
    key_value2 = every[:, 512:640]
    values01 = every[:, 256:384]
    has_tissue = tissue_row > 0.5
    low64 = iota((64, 128), 1) < HD

    acopies = {}
    zcopies = []
    chunks = (3, 2, 1, 0)

    def finish(j):
        for e in range(3):
            acopies[e, j].wait_recv()
        output_rows(chunks[j], att, wrecv, wlast, zout, low64)
        for k in range(4 * chunks[j], 4 * chunks[j] + 4):
            if k:
                to = lax.rem(z - steps[k] + NZ, NZ)
                zcopies.append(
                    go(zout.at[k], zin.at[z], zas.at[k], zar.at[k], to * NQ + q, x)
                )

    for j in range(4):
        chunk = chunks[j]
        at = chunk * 128
        query = qkv[at : at + 128]
        query01 = (query[:, 0:128].astype(F32) * (HD**-0.5)).astype(BF16)
        query2 = (query[:, 384:512].astype(F32) * (HD**-0.5)).astype(BF16)
        row = iota((128, 1), 0) + at
        n_mine = order_of(row, z)
        slide_mine = jnp.zeros((128, 1), jnp.int32)
        end = jnp.int32(0)
        for k in range(8):
            end = end + lens[k]
            slide_mine = slide_mine + jnp.where(n_mine * 128 + c >= end, 1, 0)
        base_ok = (slide_mine == slide_row) & (has_tissue | (row == iota((128, 512), 1)))
        parts = []
        for h in range(3):
            step = (jnp.int32(1) << lax.rem(3 * x + h, 4)) - 1
            allowed = base_ok & ((n_mine & step) == (n_row & step))
            sc = nt(query01 if h < 2 else query2, (key0, key1, key_value2)[h])
            sc = jnp.where(allowed, sc, NEG)
            ex = jnp.exp(sc - jnp.max(sc, axis=1, keepdims=True))
            total = jnp.sum(ex, axis=1, keepdims=True)
            parts.append(mm(ex.astype(BF16), values01 if h < 2 else key_value2) / total)
        att[x, chunk, 0:128] = jnp.where(low128, parts[0], parts[1]).astype(BF16)
        att[x, chunk, 128:192] = jnp.where(
            low64, pltpu.roll(parts[2][0:64], 64, 1), parts[2][64:128]
        ).astype(BF16)
        part = att.at[x, chunk]
        for e, to in enumerate(peers):
            acopies[e, j] = go(part, part, axs.at[e, j], axr.at[e, j], s, to)
    finish(0)
    finish(1)
    finish(2)
    finish(3)
    zin[z] = zout[0]

    for copy in gcopies + rcopies:
        copy.wait_recv()
    gown[:, 0:128] = gown[:, 0:128] + gprev[...].astype(F32)
    gown[:, 384:512] = gown[:, 384:512] + gnext[...].astype(F32)
    gfin[...] = gown[...].astype(BF16)
    total = rin[0].astype(F32)
    for g in range(1, NX):
        total = total + rin[g].astype(F32)
    rfin[...] = total[:, 0:192].astype(BF16)
    outward = [
        pltpu.make_async_copy(rfin, out_region, osem.at[1]),
        pltpu.make_async_copy(gfin, out_grad, osem.at[2]),
    ]
    for copy in outward:
        copy.start()

    for copy in zcopies:
        copy.wait_recv()
    rows_a = mm(perm_a[...], zin[:, 0:32].reshape(512, 128)).astype(BF16)
    rows_b = mm(perm_b[...], zin[:, 32:48].reshape(256, 128)).astype(BF16)
    pout[:, 0:64] = rows_a.reshape(NQ, 64, 128)
    pout[:, 64:96] = rows_b.reshape(NQ, 32, 128)
    backs = []
    for d in range(1, NQ):
        to = lax.rem(q + d, NQ)
        backs.append(go(pout.at[to], pin.at[q], pbs.at[d], pbr.at[d], z * NQ + to, x))
    own_back = pltpu.make_async_copy(pout.at[q], pin.at[q], osem.at[0])
    own_back.start()
    for copy in backs:
        copy.wait_recv()
    own_back.wait()
    for copy in outward:
        copy.wait()
    for copy in sent:
        copy.wait_send()


def blocks_of(wide, out):
    for g in range(NX):
        at = g * 192 - (g & 1) * 64
        piece = wide[:, at : at + 256]
        out[g] = (pltpu.roll(piece, 192, 1) if g & 1 else piece).astype(BF16)


def w_out_rows(wcopies, wrecv, wlast):
    for copy in wcopies:
        copy.wait_recv()
    wlast[:, 64:128] = wrecv[:, 128:192]


def output_rows(chunk, att, wrecv, wlast, zout, low64):
    acc = jnp.zeros((128, 256), F32)
    upper = jnp.zeros((64, 256), F32)
    lower = jnp.zeros((64, 256), F32)
    for g in range(NX):
        acc = acc + mm(att[g, chunk, 0:128], wrecv[g, 0:128])
        upper = upper + mm(att[g, chunk, 128:192], wlast[g, 64:192])
        lower = lower + mm(att[g, chunk, 128:192], wlast[g, 0:128])
    acc = acc + jnp.concatenate([upper, lower], axis=0)
    two = acc[:, 128:256].reshape(4, 2, 16, 128)
    packed = jnp.where(
        low64,
        two[:, 0].reshape(64, 128),
        pltpu.roll(two[:, 1].reshape(64, 128), 64, 1),
    )
    at = chunk * 4
    zout[at : at + 4, 0:32] = acc[:, 0:128].reshape(4, 32, 128).astype(BF16)
    zout[at : at + 4, 32:48] = packed.reshape(4, 16, 128).astype(BF16)


def assemble(pin, region, grad, out_tile, out_region, out_grad, rows_out):
    out_region[...] = region[...]
    out_grad[...] = grad[...]
    for p in range(NQ):
        half = pin[p, 64:96].astype(F32)
        turned = pltpu.roll(half, 64, 1)
        for i in range(4):
            at = i * 128 + p * 16
            k = (i & 1) * 16
            rows_out[at : at + 16, 0:128] = pin[p, 16 * i : 16 * i + 16].astype(F32)
            rows_out[at : at + 16, 128:256] = (half if i < 2 else turned)[k : k + 16]
    for i in range(4):
        at = i * 128
        out_tile[0:128, at : at + 128] = jnp.transpose(rows_out[at : at + 128, 0:128]).astype(BF16)
        out_tile[128:192, at : at + 128] = jnp.transpose(rows_out[at : at + 128, 128:256])[
            0:64
        ].astype(BF16)


def body(
    tile_rows,
    tissue_mask,
    slide_lengths,
    region_rows,
    parent_lists,
    child_counts,
    region_cotangent,
    w_query,
    w_key,
    w_value,
    w_output,
    w_cross_query,
    w_cross_output,
):
    dma = pltpu.SemaphoreType.DMA
    vmem = lambda *shape: pltpu.VMEM(shape, BF16)
    parts, region, grad_t = pl.pallas_call(
        kernel,
        out_shape=(
            jax.ShapeDtypeStruct((8, 96, 128), BF16),
            jax.ShapeDtypeStruct((32, 192), BF16),
            jax.ShapeDtypeStruct((192, 512), BF16),
        ),
        in_specs=[pl.BlockSpec(memory_space=pl.ANY)] * 13,
        out_specs=(pl.BlockSpec(memory_space=pl.ANY),) * 3,
        scratch_shapes=[
            vmem(512, 768),
            pltpu.VMEM((512, 128), jnp.int32),
            vmem(32, 768),
            pltpu.VMEM((16, 32), jnp.int32),
            pltpu.VMEM((1, 32), jnp.int32),
            vmem(32, 768),
            pltpu.SMEM((8,), jnp.int32),
            vmem(640, 768),
            vmem(192, 768),
            vmem(256, 768),
            vmem(192, 768),
            vmem(4, 192, 256),
            vmem(128, 768),
            vmem(16, 16, 384),
            vmem(4, 16, 16, 384),
            vmem(512, 640),
            vmem(768, 384),
            vmem(4, 192, 256),
            vmem(4, 192, 256),
            vmem(4, 4, 192, 128),
            vmem(16, 48, 128),
            vmem(16, 48, 128),
            vmem(8, 96, 128),
            vmem(32, 192),
            vmem(192, 512),
            vmem(2, 192, 128),
            pltpu.VMEM((192, 512), F32),
            vmem(192, 128),
            vmem(192, 128),
            vmem(4, 32, 256),
            vmem(4, 32, 256),
            vmem(512, 512),
            vmem(256, 256),
            dma((3,)),
            dma((16,)),
            dma((8,)),
            dma((8,)),
            dma((16,)),
            dma((16,)),
            dma((4, 8)),
            dma((4, 8)),
            dma((4,)),
            dma((4,)),
            dma((2,)),
            dma((2,)),
            dma((4, 4)),
            dma((4, 4)),
            dma((16,)),
            dma((16,)),
            dma((8,)),
            dma((8,)),
            dma((2,)),
            dma((2,)),
            dma((4,)),
            dma((4,)),
        ],
        compiler_params=pltpu.CompilerParams(
            collective_id=0, has_side_effects=True, vmem_limit_bytes=60 * 1024 * 1024
        ),
    )(
        slide_lengths,
        tile_rows,
        tissue_mask.reshape(512, 128),
        region_rows,
        parent_lists.T,
        child_counts.reshape(1, 32),
        region_cotangent,
        w_query.T,
        w_key.T,
        w_value.T,
        w_output,
        w_cross_query.T,
        w_cross_output,
    )
    tile_t, region, grad_t = pl.pallas_call(
        assemble,
        out_shape=(
            jax.ShapeDtypeStruct((192, 512), BF16),
            jax.ShapeDtypeStruct((32, 192), BF16),
            jax.ShapeDtypeStruct((192, 512), BF16),
        ),
        scratch_shapes=[pltpu.VMEM((512, 256), F32)],
    )(parts, region, grad_t)
    return tile_t.T, region, grad_t.T


def solution(mesh):
    in_specs = (
        P("seq", None),
        P(),
        P(),
        P("seq", None),
        P("seq", None),
        P("seq"),
        P("seq", None),
        P(None, "head"),
        P(None, "head"),
        P(None, "head"),
        P("head", None),
        P(None, "head"),
        P("head", None),
    )
    out_specs = (P("seq", "head"), P("seq", "head"), P("seq", "head"))
    return jax.shard_map(body, mesh=mesh, in_specs=in_specs, out_specs=out_specs, check_vma=False)
```
